32 devices in a mesh: dp: 4 (over y, core), expert: 8 (over z, x).
Axes of the slice: x: 2, y: 2, z: 4, core: 2. Of those that a mesh axis runs over, the one named last changes fastest.
Arguments:
- tokens: bfloat16 [4, 1024, 3584], P('dp', 'expert'), may hold values from -6 to 6
- cotangent: bfloat16 [4, 1024, 1024], P('dp', 'expert'), may hold values from -12 to 12
- gate_weights: float32 [4, 1024], replicated, may hold values from 0.1 to 1
- tile_expert: int32 [4, 8], replicated, may hold values from 0 to 7, as said below
- w_gate: bfloat16 [8, 3584, 1024], P('expert', None, 'dp'), may hold values from -0.09375 to 0.09375
- w_up: bfloat16 [8, 3584, 1024], P('expert', None, 'dp'), may hold values from -0.09375 to 0.09375
Outputs:
- d_tokens: bfloat16 [4, 1024, 3584], P('dp', 'expert')
- hidden: bfloat16 [4, 1024, 1024], P(None, 'expert', 'dp')
- grad_gate: bfloat16 [8, 3584, 1024], P('expert', None, 'dp')
- grad_up: bfloat16 [8, 3584, 1024], P('expert', None, 'dp')
The draws below stay inside these ranges and needn't reach their ends.
Inputs may be any that keep to these rules, and one draw needn't show every extreme that they name: tile_expert[g, j] is either j or (j + 1) mod 8: the expert of the tile's own index of the expert axis or of the next index round the closed cycle.
All inputs are finite; a program needn't handle non-finite values.
Results may differ from the reference program's by a relative error of at most 0.009.
Values may be sent and summed in bfloat16 or wider, within the bound.
No kernel may reach another device: no remote copies, remote signals or barrier semaphores. Data moves between devices by JAX's collectives and lax.ppermute only.
A program may use at most 128 MiB of HBM per device.

```python
import jax
import jax.numpy as jnp
from jax import lax

D = 3584
HID = 1024
TILE = 128
TILES_DEV = 1
GROUPS = 4
EXPERTS = 8
CYCLE_ROWS = 1024
CYCLE_TILES = 8


def draw_tile_expert(key, part):
    offsets = jax.random.randint(jax.random.fold_in(key, 11), (GROUPS, CYCLE_TILES), 0, 2)
    places = jnp.arange(CYCLE_TILES, dtype=jnp.int32) // TILES_DEV
    return ((places[None, :] + offsets) % EXPERTS).astype(jnp.int32)


def block_levels(rng, shape, shards, least, largest):
    def one(position, shards_of):
        draws = jax.random.uniform(jax.random.fold_in(jax.random.fold_in(rng, 6), position), (shards_of,), jnp.float32, least / len(shards), largest / len(shards))
        return jnp.repeat(jnp.exp(draws), shape[position] // shards_of).reshape((-1,) + (1,) * (len(shape) - position - 1))

    loudness = one(*shards[0])
    for cut in shards[1:]:
        loudness = loudness * one(*cut)
    return loudness


def gaussian(rng, shape, deviation, most, split=(), kind=jnp.bfloat16):
    loudness = block_levels(rng, shape, split, -0.22, 0.18) if split else 1.0
    drawn = jax.random.normal(rng, shape, jnp.float32) * deviation * loudness
    return jnp.minimum(jnp.maximum(drawn, -most), most).astype(kind)


def setup_inputs(seed: int = 0) -> dict:
    arg_keys = jax.random.split(jax.random.key(seed), 7)
    return {
        "tokens": gaussian(arg_keys[0], (GROUPS, CYCLE_ROWS, D), 1.0, 6.0, ((0, 4), (1, 8))),
        "cotangent": gaussian(arg_keys[1], (GROUPS, CYCLE_ROWS, HID), 2.0, 12.0, ((0, 4), (1, 8))),
        "gate_weights": jnp.clip(jax.random.uniform(arg_keys[2], (GROUPS, CYCLE_ROWS), jnp.float32, 0.1, 1.0), 0.1, 1.0),
        "tile_expert": draw_tile_expert(jax.random.fold_in(arg_keys[6], 71), 0),
        "w_gate": gaussian(arg_keys[4], (EXPERTS, D, HID), D ** -0.5, 0.09375, ((0, 8), (2, 4))),
        "w_up": gaussian(arg_keys[5], (EXPERTS, D, HID), D ** -0.5, 0.09375, ((0, 8), (2, 4))),
    }


def reference(tokens, cotangent, gate_weights, tile_expert, w_gate, w_up):
    groups = tokens.shape[0]
    cycle_count = w_gate.shape[0]
    row_count = tokens.shape[1] // cycle_count
    tile_count = row_count // TILE
    model_width = tokens.shape[2]
    quarter = HID // groups
    tile_rows = tokens.reshape(groups, cycle_count, row_count, model_width)
    tile_grads = cotangent.reshape(groups, cycle_count, row_count, HID)
    row_weights = gate_weights.reshape(groups, cycle_count, row_count)
    owners = jnp.repeat(tile_expert.reshape(groups, cycle_count, tile_count), TILE, axis=2, total_repeat_length=row_count)

    def select_at(source, slot_index):
        return lax.dynamic_index_in_dim(source, slot_index, 1, keepdims=False)

    def per_expert(expert):
        previous = (expert + cycle_count - 1) % cycle_count
        cand_rows = jnp.concatenate([select_at(tile_rows, expert), select_at(tile_rows, previous)], 1)
        cand_grads = jnp.concatenate([select_at(tile_grads, expert), select_at(tile_grads, previous)], 1)
        cand_weights = jnp.concatenate([select_at(row_weights, expert), select_at(row_weights, previous)], 1)
        cand_owners = jnp.concatenate([select_at(owners, expert), select_at(owners, previous)], 1)
        row_scale = jnp.where(cand_owners == expert, cand_weights, jnp.zeros_like(cand_weights)).reshape(-1, 1)
        flat_rows = cand_rows.reshape(-1, model_width)
        gate_panel = lax.dynamic_index_in_dim(w_gate, expert, 0, keepdims=False)
        up_panel = lax.dynamic_index_in_dim(w_up, expert, 0, keepdims=False)
        gate_val = jnp.dot(flat_rows, gate_panel, preferred_element_type=jnp.float32)
        up_val = jnp.dot(flat_rows, up_panel, preferred_element_type=jnp.float32)
        sigmoid_val = jax.nn.sigmoid(gate_val)
        activation = gate_val * sigmoid_val
        hidden_rows = (row_scale * activation * up_val).astype(jnp.bfloat16)
        act_grad = row_scale * cand_grads.reshape(-1, HID).astype(jnp.float32)
        up_grad = (act_grad * activation).astype(jnp.bfloat16)
        gate_grad = (act_grad * up_val * sigmoid_val * (1.0 + gate_val * (1.0 - sigmoid_val))).astype(jnp.bfloat16)
        row_total = jnp.zeros((flat_rows.shape[0], model_width), jnp.float32)
        for quarter_index in range(groups):
            start_col = quarter_index * quarter
            part_sum = jnp.dot(gate_grad[:, start_col:start_col + quarter], gate_panel[:, start_col:start_col + quarter].T, preferred_element_type=jnp.float32)
            part_sum = part_sum + jnp.dot(up_grad[:, start_col:start_col + quarter], up_panel[:, start_col:start_col + quarter].T, preferred_element_type=jnp.float32)
            rounded = lax.optimization_barrier(part_sum.astype(jnp.bfloat16))
            row_total = row_total + rounded.astype(jnp.float32)
        row_total = row_total.astype(jnp.bfloat16).reshape(groups, 2 * row_count, model_width)
        hidden_rows = hidden_rows.reshape(groups, 2 * row_count, HID)
        grad_gate = (jnp.dot(flat_rows.T, gate_grad, preferred_element_type=jnp.float32) / TILE).astype(jnp.bfloat16)
        grad_up = (jnp.dot(flat_rows.T, up_grad, preferred_element_type=jnp.float32) / TILE).astype(jnp.bfloat16)
        return (row_total[:, :row_count], row_total[:, row_count:], hidden_rows[:, :row_count], hidden_rows[:, row_count:], grad_gate, grad_up)

    own_rows, prev_rows, own_hidden, prev_hidden, grad_gate, grad_up = lax.map(per_expert, jnp.arange(cycle_count, dtype=jnp.int32))

    def combine(own_part, prev_part):
        joined = own_part.astype(jnp.float32) + jnp.roll(prev_part, -1, axis=0).astype(jnp.float32)
        joined = joined.astype(jnp.bfloat16)
        return jnp.transpose(joined, (1, 0, 2, 3)).reshape(groups, cycle_count * row_count, joined.shape[-1])

    return combine(own_rows, prev_rows), combine(own_hidden, prev_hidden), grad_gate, grad_up
```

```python
import functools

import jax
import jax.numpy as jnp
from jax import lax
from jax.experimental import pallas as pl
from jax.experimental.pallas import tpu as pltpu
from jax.sharding import PartitionSpec as P

TILE = 128
HEAD = 80


def shifted(value, steps):
    count = lax.axis_size("expert")
    pairs = [(source, (source + steps) % count) for source in range(count)]
    return lax.ppermute(value, "expert", pairs)


def across(value):
    count = lax.axis_size("dp")
    pairs = [(source, (source + count // 2) % count) for source in range(count)]
    return lax.ppermute(value, "dp", pairs)


def within(value):
    count = lax.axis_size("dp")
    pairs = [(source, source + 1 - 2 * (source % 2)) for source in range(count)]
    return lax.ppermute(value, "dp", pairs)


def column_step(width):
    for step in (512, 256, 128):
        if width % step == 0:
            return step
    return width


def contract(left, right, left_axis, right_axis):
    return lax.dot_general(
        left, right, (((left_axis,), (right_axis,)), ((), ())), preferred_element_type=jnp.float32
    )


def joined(refs, columns):
    return jnp.concatenate([ref[:, columns] for ref in refs], axis=0)


def block_body(piece_count, step, *refs):
    pieces = refs[:piece_count]
    scale_ref, grads_ref, gate_ref, up_ref, hidden_ref, value_grads_ref, part_ref = refs[piece_count:]
    width, quarter = gate_ref.shape
    rows = hidden_ref.shape[0]
    gate_val = jnp.zeros((rows, quarter), jnp.float32)
    up_val = jnp.zeros((rows, quarter), jnp.float32)
    for start in range(0, width, step):
        columns = pl.ds(start, step)
        values = joined(pieces, columns)
        gate_val += contract(values, gate_ref[columns, :], 1, 0)
        up_val += contract(values, up_ref[columns, :], 1, 0)
    factor = scale_ref[...]
    sigmoid_val = jax.nn.sigmoid(gate_val)
    activation = gate_val * sigmoid_val
    hidden_ref[...] = (factor * activation * up_val).astype(hidden_ref.dtype)
    act_grad = factor * grads_ref[...].astype(jnp.float32)
    up_grad = (act_grad * activation).astype(jnp.bfloat16)
    gate_grad = (act_grad * up_val * sigmoid_val * (1.0 + gate_val * (1.0 - sigmoid_val))).astype(
        jnp.bfloat16
    )
    value_grads_ref[:, :quarter] = gate_grad
    value_grads_ref[:, quarter:] = up_grad
    for start in range(0, width, step):
        columns = pl.ds(start, step)
        part_ref[:, columns] = (
            contract(gate_grad, gate_ref[columns, :], 1, 1)
            + contract(up_grad, up_ref[columns, :], 1, 1)
        ).astype(part_ref.dtype)


def block_pass(pieces, scale, grads, gate_panel, up_panel):
    rows = sum(piece.shape[0] for piece in pieces)
    width, quarter = gate_panel.shape
    return pl.pallas_call(
        functools.partial(block_body, len(pieces), column_step(width)),
        out_shape=(
            jax.ShapeDtypeStruct((rows, quarter), jnp.bfloat16),
            jax.ShapeDtypeStruct((rows, 2 * quarter), jnp.bfloat16),
            jax.ShapeDtypeStruct((rows, width), jnp.bfloat16),
        ),
        compiler_params=pltpu.CompilerParams(vmem_limit_bytes=40 * 2**20),
        cost_estimate=pl.CostEstimate(
            flops=8 * rows * width * quarter,
            bytes_accessed=4 * (rows + quarter) * width,
            transcendentals=rows * quarter,
        ),
        name="block_pass",
    )(*pieces, scale, grads, gate_panel, up_panel)


def weight_body(piece_count, grad_count, *refs):
    pieces = refs[:piece_count]
    grads = refs[piece_count : piece_count + grad_count]
    gate_out, up_out = refs[piece_count + grad_count :]
    quarter = gate_out.shape[1]
    values = joined(pieces, slice(None))
    value_grads = joined(grads, slice(None))
    total = contract(values, value_grads, 0, 0) * (1.0 / TILE)
    gate_out[...] = total[:, :quarter].astype(gate_out.dtype)
    up_out[...] = total[:, quarter:].astype(up_out.dtype)


def weight_pass(pieces, grads):
    width = pieces[0].shape[1]
    quarter = grads[0].shape[1] // 2
    step = column_step(width)
    rows = sum(piece.shape[0] for piece in pieces)
    return pl.pallas_call(
        functools.partial(weight_body, len(pieces), len(grads)),
        grid=(width // step,),
        in_specs=[pl.BlockSpec((piece.shape[0], step), lambda i: (0, i)) for piece in pieces]
        + [pl.BlockSpec(grad.shape, lambda i: (0, 0)) for grad in grads],
        out_specs=[pl.BlockSpec((step, quarter), lambda i: (i, 0))] * 2,
        out_shape=[jax.ShapeDtypeStruct((width, quarter), jnp.bfloat16)] * 2,
        compiler_params=pltpu.CompilerParams(vmem_limit_bytes=40 * 2**20),
        cost_estimate=pl.CostEstimate(
            flops=4 * rows * width * quarter,
            bytes_accessed=2 * rows * width + 4 * quarter * width,
            transcendentals=0,
        ),
        name="weight_pass",
    )(*pieces, *grads)


def route_scale(tile_expert, gate_weights, source, expert, row_count):
    tile_count = row_count // TILE
    owners = lax.dynamic_slice_in_dim(tile_expert, source * tile_count, tile_count, 1)
    weights = lax.dynamic_slice_in_dim(gate_weights, source * row_count, row_count, 1)
    routed = jnp.repeat(owners == expert, TILE, axis=1, total_repeat_length=row_count)
    return jnp.where(routed, weights, jnp.zeros_like(weights))


def relative(value, side, core):
    flipped = jnp.where(core == 1, value[jnp.array([1, 0, 3, 2])], value)
    return jnp.where(side == 1, flipped[jnp.array([2, 3, 0, 1])], flipped)


def f32(value):
    return value.astype(jnp.float32)


def b16(value):
    return value.astype(jnp.bfloat16)


def per_device(tokens, cotangent, gate_weights, tile_expert, w_gate, w_up):
    row_count = tokens.shape[1]
    cycle_size = lax.axis_size("expert")
    position = lax.axis_index("expert")
    rank = lax.axis_index("dp")
    side, core = rank // 2, rank % 2
    gate_panel, up_panel = w_gate[0], w_up[0]
    quarter = gate_panel.shape[1]
    head = HEAD * row_count // TILE
    tile, tile_grad = tokens[0], cotangent[0]
    top, low = tile[:head], tile[head:]

    y_low = across(low)
    x_top = shifted(top, 1)
    grad_sent = lax.dynamic_slice_in_dim(tile_grad, (1 - side) * 2 * quarter, 2 * quarter, 1)
    grad_kept = lax.dynamic_slice_in_dim(tile_grad, side * 2 * quarter, 2 * quarter, 1)
    grad_got = across(grad_sent)
    y_top = across(top)
    x_low = shifted(low, 1)
    c_tile = within(tile)
    both = jnp.stack([grad_kept, grad_got])
    both_kept = lax.dynamic_slice_in_dim(both, core * quarter, quarter, 2)
    both_got = within(lax.dynamic_slice_in_dim(both, (1 - core) * quarter, quarter, 2))
    home_grads = jnp.stack([both_kept, both_got], axis=1).reshape(2, 2 * row_count, quarter)
    past_grads = shifted(home_grads, 1)
    xy_low = shifted(y_low, 1)
    xy_top = across(x_top)
    cy_low, cy_top = within(y_low), within(y_top)
    cx_top, cx_low = within(x_top), within(x_low)
    cxy_low, cxy_top = within(xy_low), within(xy_top)

    before = (position + cycle_size - 1) % cycle_size
    home_scale = relative(
        route_scale(tile_expert, gate_weights, position, position, row_count), side, core
    ).reshape(2, 2 * row_count, 1)
    past_scale = relative(
        route_scale(tile_expert, gate_weights, before, position, row_count), side, core
    ).reshape(2, 2 * row_count, 1)

    home_near = (tile, c_tile)
    home_far = (y_top, y_low, cy_top, cy_low)
    past_near = (x_top, x_low, cx_top, cx_low)
    past_far = (xy_top, xy_low, cxy_top, cxy_low)
    panels = (gate_panel, up_panel)
    hid_hn, vg_hn, part_hn = block_pass(home_near, home_scale[0], home_grads[0], *panels)
    hid_hf, vg_hf, part_hf = block_pass(home_far, home_scale[1], home_grads[1], *panels)
    hid_pn, vg_pn, part_pn = block_pass(past_near, past_scale[0], past_grads[0], *panels)
    hid_pf, vg_pf, part_pf = block_pass(past_far, past_scale[1], past_grads[1], *panels)

    def pair_sum(part):
        return b16(f32(part[:row_count]) + f32(within(part[row_count:])))

    pair_hn, pair_hf = pair_sum(part_hn), pair_sum(part_hf)
    pair_pn, pair_pf = pair_sum(part_pn), pair_sum(part_pf)
    hid_back = shifted(jnp.stack([hid_pn, hid_pf]), -1)
    low_near = shifted(pair_pn[head:], -1)
    low_far = shifted(pair_pf[head:], -1)
    top_home = across(pair_hf[:head])
    top_past = across(pair_pf[:head])
    top_back = shifted(b16(f32(pair_pn[:head]) + f32(top_past)), -1)
    low_home = across(b16(f32(pair_hf[head:]) + f32(low_far)))
    d_top = f32(pair_hn[:head]) + f32(top_home) + f32(top_back)
    d_low = f32(pair_hn[head:]) + f32(low_near) + f32(low_home)
    d_tokens = b16(jnp.concatenate([d_top, d_low], axis=0))[None]

    hidden = b16(f32(jnp.stack([hid_hn, hid_hf])) + f32(hid_back))
    hidden = relative(hidden.reshape(4, row_count, quarter), side, core)
    grad_gate, grad_up = weight_pass(
        home_near + home_far + past_near + past_far, (vg_hn, vg_hf, vg_pn, vg_pf)
    )
    return (d_tokens, hidden, grad_gate[None], grad_up[None])


def solution(mesh):
    in_specs = (
        P("dp", "expert", None),
        P("dp", "expert", None),
        P(),
        P(),
        P("expert", None, "dp"),
        P("expert", None, "dp"),
    )
    out_specs = (
        P("dp", "expert", None),
        P(None, "expert", "dp"),
        P("expert", None, "dp"),
        P("expert", None, "dp"),
    )
    return jax.shard_map(
        per_device, mesh=mesh, in_specs=in_specs, out_specs=out_specs, check_vma=False
    )
```

```python
import functools

import jax
import jax.numpy as jnp
from jax import lax
from jax.experimental import pallas as pl
from jax.experimental.pallas import tpu as pltpu
from jax.sharding import PartitionSpec as P

TILE = 128
OUT_SHARE = 64
BACK_SHARE = (48, 80)
LIMIT = 28 * 2**20
COST = pl.CostEstimate(flops=10**12, bytes_accessed=10**9, transcendentals=0)


def shifted(value, steps):
    count = lax.axis_size("expert")
    pairs = [(source, (source + steps) % count) for source in range(count)]
    return lax.ppermute(value, "expert", pairs)


def across(value):
    count = lax.axis_size("dp")
    pairs = [(source, (source + count // 2) % count) for source in range(count)]
    return lax.ppermute(value, "dp", pairs)


def within(value):
    count = lax.axis_size("dp")
    pairs = [(source, source + 1 - 2 * (source % 2)) for source in range(count)]
    return lax.ppermute(value, "dp", pairs)


def after(values, *earlier):
    return lax.optimization_barrier((values, earlier))[0]


def f32(value):
    return value.astype(jnp.float32)


def b16(value):
    return value.astype(jnp.bfloat16)


def column_step(width):
    for step in (512, 256, 128):
        if width % step == 0:
            return step
    return width


def contract(left, right, left_axis, right_axis):
    return lax.dot_general(
        left, right, (((left_axis,), (right_axis,)), ((), ())), preferred_element_type=jnp.float32
    )


def joined(refs, columns):
    return jnp.concatenate([ref[:, columns] for ref in refs], axis=0)


def block_body(piece_count, grad_count, step, *refs):
    pieces, refs = refs[:piece_count], refs[piece_count:]
    grad_refs, refs = refs[:grad_count], refs[grad_count:]
    scale_ref, *panels = refs[:5]
    hidden_ref, own_ref, other_ref, *refs = refs[5:]
    *part_refs, values_ref, panels_ref, piece_sems, panel_sems = refs
    rows, width = values_ref.shape
    quarter = panels_ref.shape[2]
    chunks = width // step

    copies = []
    first = 0
    for index, piece in enumerate(pieces):
        target = values_ref.at[pl.ds(first, piece.shape[0]), :]
        copies.append(pltpu.make_async_copy(piece, target, piece_sems.at[index]))
        first += piece.shape[0]
    loads = []
    for chunk in range(chunks):
        columns = pl.ds(chunk * step, step)
        loads.append(
            [
                pltpu.make_async_copy(
                    panel.at[columns, :], panels_ref.at[which, columns, :], panel_sems.at[which, chunk]
                )
                for which, panel in enumerate(panels)
            ]
        )
    for copy in copies:
        copy.start()
    for load in loads:
        for copy in load:
            copy.start()
    for copy in copies:
        copy.wait()

    sums = [jnp.zeros((rows, quarter), jnp.float32) for _ in panels]
    for chunk in range(chunks):
        columns = pl.ds(chunk * step, step)
        for copy in loads[chunk]:
            copy.wait()
        values = values_ref[:, columns]
        sums = [
            total + contract(values, panels_ref[which, columns, :], 1, 0)
            for which, total in enumerate(sums)
        ]
    factor = scale_ref[...]
    grads = []
    for which, out_ref in enumerate((own_ref, other_ref)):
        gate_val, up_val = sums[2 * which : 2 * which + 2]
        columns = pl.ds(which * quarter, quarter)
        sigmoid_val = jax.nn.sigmoid(gate_val)
        activation = gate_val * sigmoid_val
        hidden_ref[:, columns] = b16(factor * activation * up_val)
        act_grad = factor * f32(joined(grad_refs, columns))
        up_grad = b16(act_grad * activation)
        gate_grad = b16(act_grad * up_val * sigmoid_val * (1.0 + gate_val * (1.0 - sigmoid_val)))
        out_ref[:, :quarter] = gate_grad
        out_ref[:, quarter:] = up_grad
        grads += [gate_grad, up_grad]
    for chunk in range(chunks):
        columns = pl.ds(chunk * step, step)
        part = b16(
            sum(
                contract(grad, panels_ref[which, columns, :], 1, 1)
                for which, grad in enumerate(grads)
            )
        )
        first = 0
        for part_ref in part_refs:
            part_ref[:, columns] = part[first : first + part_ref.shape[0]]
            first += part_ref.shape[0]


def block_pass(pieces, grads, scale, panels, part_rows):
    rows = sum(piece.shape[0] for piece in pieces)
    width, quarter = panels[0].shape
    step = column_step(width)
    wide = jax.ShapeDtypeStruct((rows, 2 * quarter), jnp.bfloat16)
    here, there = pl.BlockSpec(memory_space=pltpu.VMEM), pl.BlockSpec(memory_space=pl.ANY)
    hidden, own, other, *parts = pl.pallas_call(
        functools.partial(block_body, len(pieces), len(grads), step),
        out_shape=[wide] * 3
        + [jax.ShapeDtypeStruct((count, width), jnp.bfloat16) for count in part_rows],
        in_specs=[there] * len(pieces) + [here] * (len(grads) + 1) + [there] * 4,
        out_specs=[here] * (3 + len(part_rows)),
        scratch_shapes=[
            pltpu.VMEM((rows, width), jnp.bfloat16),
            pltpu.VMEM((4, width, quarter), jnp.bfloat16),
            pltpu.SemaphoreType.DMA((len(pieces),)),
            pltpu.SemaphoreType.DMA((4, width // step)),
        ],
        compiler_params=pltpu.CompilerParams(vmem_limit_bytes=LIMIT),
        cost_estimate=COST,
        name="block_pass",
    )(*pieces, *grads, scale, *panels)
    return hidden, own, other, parts


def weight_body(piece_count, grad_count, *refs):
    pieces = refs[:piece_count]
    grads = refs[piece_count : piece_count + grad_count]
    gate_ref, up_ref = refs[piece_count + grad_count :]
    quarter = gate_ref.shape[1]
    total = contract(joined(pieces, slice(None)), joined(grads, slice(None)), 0, 0)
    total = b16(total * (1.0 / TILE))
    gate_ref[...] = total[:, :quarter]
    up_ref[...] = total[:, quarter:]


def weight_pass(pieces, grads, width):
    quarter = grads[0].shape[1] // 2
    step = column_step(width)
    return pl.pallas_call(
        functools.partial(weight_body, len(pieces), len(grads)),
        grid=(width // step,),
        in_specs=[pl.BlockSpec((piece.shape[0], step), lambda i: (0, i)) for piece in pieces]
        + [pl.BlockSpec(grad.shape, lambda i: (0, 0)) for grad in grads],
        out_specs=[pl.BlockSpec((step, quarter), lambda i: (i, 0))] * 2,
        out_shape=[jax.ShapeDtypeStruct((width, quarter), jnp.bfloat16)] * 2,
        compiler_params=pltpu.CompilerParams(vmem_limit_bytes=LIMIT),
        cost_estimate=COST,
        name="weight_pass",
    )(*pieces, *grads)


def hidden_body(rank_ref, own_ref, got_ref, out_ref):
    for block in range(2):
        group = 2 * block
        out_ref[group ^ rank_ref[0]] = own_ref[block]
        out_ref[(group + 1) ^ rank_ref[0]] = got_ref[block]


def hidden_pass(rank, own, got):
    blocks, rows, quarter = own.shape
    return pl.pallas_call(
        hidden_body,
        out_shape=jax.ShapeDtypeStruct((2 * blocks, rows, quarter), own.dtype),
        in_specs=[pl.BlockSpec(memory_space=pltpu.SMEM)] + [pl.BlockSpec(memory_space=pltpu.VMEM)] * 2,
        cost_estimate=COST,
        name="hidden_pass",
    )(rank.reshape(1), own, got)


def total_body(*refs):
    base_ref, *part_refs, out_ref = refs
    first = 0
    for part_ref in part_refs:
        rows = pl.ds(first, part_ref.shape[0])
        out_ref[rows, :] = b16(f32(base_ref[rows, :]) + f32(part_ref[...]))
        first += part_ref.shape[0]


def total(base, *parts):
    return pl.pallas_call(
        total_body,
        out_shape=jax.ShapeDtypeStruct(base.shape, base.dtype),
        compiler_params=pltpu.CompilerParams(vmem_limit_bytes=LIMIT),
        cost_estimate=COST,
        name="total",
    )(base, *parts)


def per_device(tokens, cotangent, gate_weights, tile_expert, w_gate, w_up):
    row_count = tokens.shape[1]
    tile_count = row_count // TILE
    cycle_size = lax.axis_size("expert")
    position = lax.axis_index("expert")
    before = (position + cycle_size - 1) % cycle_size
    group_count = lax.axis_size("dp")
    rank = lax.axis_index("dp")
    side, core = rank // 2, rank % 2
    quarter = w_gate.shape[2]
    out_head = OUT_SHARE * tile_count
    mid, head = (share * tile_count for share in BACK_SHARE)
    tile, tile_grad = tokens[0], cotangent[0]

    def row_scale(group, place):
        owners = lax.dynamic_slice(tile_expert, (group, place * tile_count), (1, tile_count))
        weights = lax.dynamic_slice(gate_weights, (group, place * row_count), (1, row_count))
        routed = jnp.repeat(owners == position, TILE, axis=1, total_repeat_length=row_count)
        return jnp.where(routed, weights, jnp.zeros_like(weights)).reshape(row_count, 1)

    def side_grads(which):
        return jnp.concatenate(
            [
                lax.dynamic_slice_in_dim(tile_grad, (2 * which + first) * quarter, quarter, 1)
                for first in (core, 1 - core)
            ],
            axis=1,
        )

    far = (rank + group_count // 2) % group_count
    scale_hn = row_scale(rank, position)
    scale_hf = row_scale(far, position)
    scale_pn = row_scale(rank, before)
    scale_pf = row_scale(far, before)

    grads, grads_sent = side_grads(side), side_grads(1 - side)
    x_tile, x_grads = shifted(tile, 1), shifted(grads, 1)
    y_tile, y_grads = across(tile), across(grads_sent)
    panels = (w_gate[0], w_up[0], within(w_gate[0]), within(w_up[0]))
    hid_hn, own_hn, other_hn, (part_hn,) = block_pass(
        (tile,), (grads,), scale_hn, panels, (row_count,)
    )
    x_tile, y_tile, x_grads, y_grads = after((x_tile, y_tile, x_grads, y_grads), hid_hn)
    xy_top = across(x_tile[:out_head])
    xy_low = shifted(y_tile[out_head:], 1)
    xy_grads = shifted(y_grads, 1)

    upper, middle, lower = mid, head - mid, row_count - head
    hid_mid, own_mid, other_mid, mid_parts = block_pass(
        (y_tile, x_tile),
        (y_grads, x_grads),
        jnp.concatenate([scale_hf, scale_pn]),
        panels,
        (upper, middle, lower, upper, middle, lower),
    )
    upper_hf, middle_hf, lower_hf, upper_pn, middle_pn, lower_pn = mid_parts
    up_home = across(upper_hf)
    mid_home = across(middle_hf)
    low_near = shifted(lower_pn, -1)
    xy_low, xy_top, xy_grads = after((xy_low, xy_top, xy_grads), hid_mid)
    hid_pf, own_pf, other_pf, (upper_pf, middle_pf, lower_pf) = block_pass(
        (xy_top, xy_low), (xy_grads,), scale_pf, panels, (upper, middle, lower)
    )
    low_far = shifted(lower_pf, -1)
    up_past = across(upper_pf)
    mid_past = across(middle_pf)
    hid_back = shifted(jnp.stack([hid_mid[row_count:], hid_pf]), -1)

    pieces = (tile, y_tile, x_tile, xy_top, xy_low)
    far_pieces = tuple(within(piece) for piece in pieces)
    far_grads = tuple(within(grad) for grad in (other_hn, other_mid, other_pf))
    grad_gate, grad_up = weight_pass(
        pieces + far_pieces,
        after((own_hn, own_mid, own_pf) + far_grads, up_home, low_near),
        tile.shape[1],
    )

    up_past, mid_past, low_far, hid_back = after((up_past, mid_past, low_far, hid_back), grad_gate)
    up_back = shifted(b16(f32(upper_pn) + f32(up_past)), -1)
    mid_back = shifted(b16(f32(middle_pn) + f32(mid_past)), -1)
    low_home = across(b16(f32(lower_hf) + f32(low_far)))
    base = total(part_hn, up_home, mid_home, low_near)
    hidden = b16(f32(jnp.stack([hid_hn, hid_mid[:row_count]])) + f32(hid_back))
    hidden = hidden_pass(rank, hidden[:, :, :quarter], within(hidden[:, :, quarter:]))
    d_tokens = total(base, up_back, mid_back, low_home)
    return (d_tokens[None], hidden, grad_gate[None], grad_up[None])


def solution(mesh):
    in_specs = (
        P("dp", "expert", None),
        P("dp", "expert", None),
        P(),
        P(),
        P("expert", None, "dp"),
        P("expert", None, "dp"),
    )
    out_specs = (
        P("dp", "expert", None),
        P(None, "expert", "dp"),
        P("expert", None, "dp"),
        P("expert", None, "dp"),
    )
    return jax.shard_map(
        per_device, mesh=mesh, in_specs=in_specs, out_specs=out_specs, check_vma=False
    )
```

```python
import functools

import jax
import jax.numpy as jnp
from jax import lax
from jax.experimental import pallas as pl
from jax.experimental.pallas import tpu as pltpu
from jax.sharding import PartitionSpec as P

TILE = 128
OUT_SHARE = 80
BACK_SHARE = (32, 48, 80)
LIMIT = 20 * 2**20
LONG = pl.CostEstimate(flops=10**12, bytes_accessed=10**9, transcendentals=0)


def work(flops, moved):
    return pl.CostEstimate(flops=flops, bytes_accessed=moved, transcendentals=0)


def shifted(value, steps):
    count = lax.axis_size("expert")
    pairs = [(source, (source + steps) % count) for source in range(count)]
    return lax.ppermute(value, "expert", pairs)


def across(value):
    count = lax.axis_size("dp")
    pairs = [(source, (source + count // 2) % count) for source in range(count)]
    return lax.ppermute(value, "dp", pairs)


def within(value):
    count = lax.axis_size("dp")
    pairs = [(source, source + 1 - 2 * (source % 2)) for source in range(count)]
    return lax.ppermute(value, "dp", pairs)


def after(values, *earlier):
    return lax.optimization_barrier((values, earlier))[0]


def f32(value):
    return value.astype(jnp.float32)


def b16(value):
    return value.astype(jnp.bfloat16)


def column_step(width):
    for step in (512, 256, 128):
        if width % step == 0:
            return step
    return width


def contract(left, right, left_axis, right_axis):
    return lax.dot_general(
        left, right, (((left_axis,), (right_axis,)), ((), ())), preferred_element_type=jnp.float32
    )


def joined(refs, columns):
    return jnp.concatenate([ref[:, columns] for ref in refs], axis=0)


def pack_body(tile_ref, grads_ref, top_ref, low_ref, far_ref):
    rank = lax.axis_index("dp")
    side, core = rank // 2, rank % 2
    width = tile_ref.shape[1]
    quarter = grads_ref.shape[1] // 4
    head, both = top_ref.shape[0], 2 * quarter
    parts = [
        grads_ref[:, pl.ds(pl.multiple_of((2 * which + first) * quarter, quarter), quarter)]
        for which in (1 - side, side)
        for first in (core, 1 - core)
    ]
    sent, kept = jnp.concatenate(parts[:2], axis=1), jnp.concatenate(parts[2:], axis=1)
    tile = tile_ref[...]
    far_ref[:, :width] = tile
    far_ref[:, width:] = sent
    for out_ref, rows in ((top_ref, slice(0, head)), (low_ref, slice(head, tile.shape[0]))):
        out_ref[:, :width] = tile[rows]
        out_ref[:, width : width + both] = sent[rows]
        out_ref[:, width + both :] = kept[rows]


def pack(tile, grads, head):
    rows, width = tile.shape
    whole = grads.shape[1]
    return pl.pallas_call(
        pack_body,
        out_shape=[
            jax.ShapeDtypeStruct((head, width + whole), tile.dtype),
            jax.ShapeDtypeStruct((rows - head, width + whole), tile.dtype),
            jax.ShapeDtypeStruct((rows, width + whole // 2), tile.dtype),
        ],
        compiler_params=pltpu.CompilerParams(vmem_limit_bytes=LIMIT),
        cost_estimate=work(0, 4 * rows * (width + whole)),
        name="pack",
    )(
        pltpu.with_memory_space_constraint(tile, pltpu.HBM),
        pltpu.with_memory_space_constraint(grads, pltpu.HBM),
    )


def block_body(grad_starts, scale_start, step, *refs):
    pieces, refs = refs[: len(grad_starts)], refs[len(grad_starts) :]
    scale_ref, *panels = refs[:5]
    hidden_ref, own_ref, other_ref, *part_refs = refs[5:]
    width, quarter = panels[0].shape
    values = joined(pieces, pl.ds(0, width))
    factor = scale_ref[pl.ds(scale_start, hidden_ref.shape[0]), :]
    grads = []
    for which, out_ref in enumerate((own_ref, other_ref)):
        gate_val = contract(values, panels[2 * which][...], 1, 0)
        up_val = contract(values, panels[2 * which + 1][...], 1, 0)
        columns = pl.ds(which * quarter, quarter)
        sigmoid_val = jax.nn.sigmoid(gate_val)
        activation = gate_val * sigmoid_val
        hidden_ref[:, columns] = b16(factor * activation * up_val)
        received = jnp.concatenate(
            [
                piece[:, pl.ds(start + which * quarter, quarter)]
                for piece, start in zip(pieces, grad_starts)
            ]
        )
        act_grad = factor * f32(received)
        up_grad = b16(act_grad * activation)
        gate_grad = b16(act_grad * up_val * sigmoid_val * (1.0 + gate_val * (1.0 - sigmoid_val)))
        out_ref[:, :quarter] = gate_grad
        out_ref[:, quarter:] = up_grad
        grads += [gate_grad.T, up_grad.T]
    for start in range(0, width, step):
        columns = pl.ds(start, step)
        part = b16(
            sum(contract(panel[columns, :], grad, 1, 0) for panel, grad in zip(panels, grads))
        ).T
        first = 0
        for part_ref in part_refs:
            part_ref[:, columns] = part[first : first + part_ref.shape[0]]
            first += part_ref.shape[0]


def block_pass(pieces, grad_starts, scales, scale_start, panels, part_rows):
    rows = sum(piece.shape[0] for piece in pieces)
    width, quarter = panels[0].shape
    wide = jax.ShapeDtypeStruct((rows, 2 * quarter), jnp.bfloat16)
    hidden, own, other, *parts = pl.pallas_call(
        functools.partial(block_body, grad_starts, scale_start, column_step(width)),
        out_shape=[wide] * 3
        + [jax.ShapeDtypeStruct((count, width), jnp.bfloat16) for count in part_rows],
        compiler_params=pltpu.CompilerParams(vmem_limit_bytes=LIMIT),
        cost_estimate=work(16 * rows * width * quarter, 4 * rows * width),
        name="block_pass",
    )(*pieces, scales, *panels)
    return hidden, own, other, parts


def weight_body(piece_count, grad_count, *refs):
    pieces = refs[:piece_count]
    grads = refs[piece_count : piece_count + grad_count]
    others = refs[piece_count + grad_count :]
    total = contract(joined(pieces, slice(None)), joined(grads, slice(None)), 0, 0)
    if len(others) == 1:
        others[0][...] = b16(total)
    else:
        got_ref, gate_ref, up_ref = others
        quarter = gate_ref.shape[1]
        total = b16((total + f32(got_ref[...])) * (1.0 / TILE))
        gate_ref[...] = total[:, :quarter]
        up_ref[...] = total[:, quarter:]


def weight_pass(width, pieces, grads, got=None):
    both = grads[0].shape[1]
    rows = sum(piece.shape[0] for piece in pieces)
    step = column_step(width)
    widths = [both] if got is None else [both // 2] * 2
    return pl.pallas_call(
        functools.partial(weight_body, len(pieces), len(grads)),
        grid=(width // step,),
        in_specs=[pl.BlockSpec((piece.shape[0], step), lambda i: (0, i)) for piece in pieces]
        + [pl.BlockSpec(grad.shape, lambda i: (0, 0)) for grad in grads]
        + ([] if got is None else [pl.BlockSpec((step, both), lambda i: (i, 0))]),
        out_specs=[pl.BlockSpec((step, columns), lambda i: (i, 0)) for columns in widths],
        out_shape=[jax.ShapeDtypeStruct((width, columns), jnp.bfloat16) for columns in widths],
        compiler_params=pltpu.CompilerParams(vmem_limit_bytes=LIMIT),
        cost_estimate=work(2 * rows * width * both, 2 * width * (rows + 2 * both)),
        name="weight_pass",
    )(*pieces, *grads, *([] if got is None else [got]))


def hidden_body(rank_ref, own_ref, got_ref, out_ref):
    for block in range(2):
        group = 2 * block
        out_ref[group ^ rank_ref[0]] = own_ref[block]
        out_ref[(group + 1) ^ rank_ref[0]] = got_ref[block]


def hidden_pass(rank, own, got):
    blocks, rows, quarter = own.shape
    return pl.pallas_call(
        hidden_body,
        out_shape=jax.ShapeDtypeStruct((2 * blocks, rows, quarter), own.dtype),
        in_specs=[pl.BlockSpec(memory_space=pltpu.SMEM)] + [pl.BlockSpec(memory_space=pltpu.VMEM)] * 2,
        cost_estimate=LONG,
        name="hidden_pass",
    )(rank.reshape(1), own, got)


def total_body(*refs):
    base_ref, *part_refs, out_ref = refs
    first = 0
    for part_ref in part_refs:
        rows = pl.ds(first, part_ref.shape[0])
        out_ref[rows, :] = b16(f32(base_ref[rows, :]) + f32(part_ref[...]))
        first += part_ref.shape[0]


def total(base, *parts):
    return pl.pallas_call(
        total_body,
        out_shape=jax.ShapeDtypeStruct(base.shape, base.dtype),
        compiler_params=pltpu.CompilerParams(vmem_limit_bytes=LIMIT),
        cost_estimate=LONG,
        name="total",
    )(base, *parts)


def per_device(tokens, cotangent, gate_weights, tile_expert, w_gate, w_up):
    row_count = tokens.shape[1]
    tile_count = row_count // TILE
    cycle_size = lax.axis_size("expert")
    position = lax.axis_index("expert")
    before = (position + cycle_size - 1) % cycle_size
    group_count = lax.axis_size("dp")
    rank = lax.axis_index("dp")
    quarter = w_gate.shape[2]
    out_head = OUT_SHARE * tile_count
    first, mid, head = (share * tile_count for share in BACK_SHARE)
    tile, tile_grad = tokens[0], cotangent[0]

    def row_scale(group, place):
        owners = lax.dynamic_slice(tile_expert, (group, place * tile_count), (1, tile_count))
        weights = lax.dynamic_slice(gate_weights, (group, place * row_count), (1, row_count))
        routed = jnp.repeat(owners == position, TILE, axis=1, total_repeat_length=row_count)
        return jnp.where(routed, weights, jnp.zeros_like(weights)).reshape(row_count, 1)

    far = (rank + group_count // 2) % group_count
    scales = jnp.concatenate(
        [
            row_scale(group, place)
            for group, place in ((rank, position), (far, position), (rank, before), (far, before))
        ]
    )

    width = tile.shape[1]
    sent_at, kept_at = width, width + 2 * quarter
    near_top, near_low, far_message = pack(tile, tile_grad, out_head)
    x_top, x_low, y_tile = shifted(near_top, 1), shifted(near_low, 1), across(far_message)
    panels = (w_gate[0], w_up[0], within(w_gate[0]), within(w_up[0]))
    hid_hn, own_hn, other_hn, (part_hn,) = block_pass(
        (near_top, near_low), (kept_at, kept_at), scales, 0, panels, (row_count,)
    )
    x_top = after(x_top, hid_hn)
    x_sent = x_top[:, :kept_at]
    xy_top = across(x_sent)
    y_tile = after(y_tile, x_sent)
    y_sent = y_tile[out_head:]
    xy_low = shifted(y_sent, 1)
    x_low = after(x_low, y_sent)

    upper, middle, lower = mid, head - mid, row_count - head
    hid_mid, own_mid, other_mid, mid_parts = block_pass(
        (y_tile, x_top, x_low),
        (sent_at, kept_at, kept_at),
        scales,
        row_count,
        panels,
        (first, head - first, lower, upper, middle, lower),
    )
    first_hf, rest_hf, lower_hf, upper_pn, middle_pn, lower_pn = mid_parts
    first_home = across(first_hf)
    low_near = shifted(lower_pn, -1)
    xy_low, xy_top = after((xy_low, xy_top), hid_mid)
    hid_pf, own_pf, other_pf, (upper_pf, middle_pf, lower_pf) = block_pass(
        (xy_top, xy_low), (sent_at, sent_at), scales, 3 * row_count, panels, (upper, middle, lower)
    )
    low_far = shifted(lower_pf, -1)
    up_past, mid_past = across(upper_pf), across(middle_pf)
    hid_back = shifted(jnp.stack([hid_mid[row_count:], hid_pf]), -1)

    pieces = (near_top, near_low, y_tile, x_top, x_low, xy_top, xy_low)
    (sent,) = weight_pass(width, pieces, after((other_hn, other_mid, other_pf), first_home, low_near))
    got = within(sent)
    up_past, rest_hf = after((up_past, rest_hf), sent)
    rest_home = across(rest_hf)
    up_sum = b16(f32(upper_pn) + f32(up_past))
    up_back = shifted(up_sum, -1)
    mid_past, low_far, hid_back = after((mid_past, low_far, hid_back), up_sum)
    mid_sum = b16(f32(middle_pn) + f32(mid_past))
    mid_back = shifted(mid_sum, -1)
    low_sum = b16(f32(lower_hf) + f32(low_far))
    low_home = across(low_sum)
    hidden = b16(f32(jnp.stack([hid_hn, hid_mid[:row_count]])) + f32(hid_back))
    hidden = hidden_pass(rank, hidden[:, :, :quarter], within(hidden[:, :, quarter:]))
    got = after(got, hidden, mid_sum, low_sum)
    grad_gate, grad_up = weight_pass(width, pieces, (own_hn, own_mid, own_pf), got)
    base = total(after(part_hn, grad_gate), first_home, rest_home, low_near)
    d_tokens = total(base, up_back, mid_back, low_home)
    return (d_tokens[None], hidden, grad_gate[None], grad_up[None])


def solution(mesh):
    in_specs = (
        P("dp", "expert", None),
        P("dp", "expert", None),
        P(),
        P(),
        P("expert", None, "dp"),
        P("expert", None, "dp"),
    )
    out_specs = (
        P("dp", "expert", None),
        P(None, "expert", "dp"),
        P("expert", None, "dp"),
        P("expert", None, "dp"),
    )
    return jax.shard_map(
        per_device, mesh=mesh, in_specs=in_specs, out_specs=out_specs, check_vma=False
    )
```

```python
import functools

import jax
import jax.numpy as jnp
from jax import lax
from jax.experimental import pallas as pl
from jax.experimental.pallas import tpu as pltpu
from jax.sharding import PartitionSpec as P

TILE = 128
OUT_SHARE = 80
BACK_SHARE = (48, 64)
LIMIT = 20 * 2**20
LONG = pl.CostEstimate(flops=10**12, bytes_accessed=10**9, transcendentals=0)


def work(flops, moved):
    return pl.CostEstimate(flops=flops, bytes_accessed=moved, transcendentals=0)


def shifted(value, steps):
    count = lax.axis_size("expert")
    pairs = [(source, (source + steps) % count) for source in range(count)]
    return lax.ppermute(value, "expert", pairs)


def across(value):
    count = lax.axis_size("dp")
    pairs = [(source, (source + count // 2) % count) for source in range(count)]
    return lax.ppermute(value, "dp", pairs)


def within(value):
    count = lax.axis_size("dp")
    pairs = [(source, source + 1 - 2 * (source % 2)) for source in range(count)]
    return lax.ppermute(value, "dp", pairs)


def after(values, *earlier):
    return lax.optimization_barrier((values, earlier))[0]


def f32(value):
    return value.astype(jnp.float32)


def b16(value):
    return value.astype(jnp.bfloat16)


def column_step(width):
    for step in (512, 256, 128):
        if width % step == 0:
            return step
    return width


def contract(left, right, left_axis, right_axis):
    return lax.dot_general(
        left, right, (((left_axis,), (right_axis,)), ((), ())), preferred_element_type=jnp.float32
    )


def joined(refs, columns):
    return jnp.concatenate([ref[:, columns] for ref in refs], axis=0)


def pack_body(tile_ref, grads_ref, top_ref, low_ref, far_ref):
    rank = lax.axis_index("dp")
    side, core = rank // 2, rank % 2
    width = tile_ref.shape[1]
    quarter = grads_ref.shape[1] // 4
    head, both = top_ref.shape[0], 2 * quarter
    top, low = slice(0, head), slice(head, tile_ref.shape[0])
    parts = [
        grads_ref[:, pl.ds(pl.multiple_of((2 * which + first) * quarter, quarter), quarter)]
        for which in (1 - side, side)
        for first in (core, 1 - core)
    ]
    sent, kept = jnp.concatenate(parts[:2], axis=1), jnp.concatenate(parts[2:], axis=1)
    tile = tile_ref[...]
    far_ref[:, :width] = tile
    far_ref[:, width:] = sent
    top_ref[:, :width] = tile[top]
    top_ref[:, width : width + both] = sent[top]
    top_ref[:, width + both :] = kept[top]
    low_ref[:, :width] = tile[low]
    low_ref[:, width:] = kept[low]


def pack(tile, grads, head):
    rows, width = tile.shape
    whole = grads.shape[1]
    return pl.pallas_call(
        pack_body,
        out_shape=[
            jax.ShapeDtypeStruct((head, width + whole), tile.dtype),
            jax.ShapeDtypeStruct((rows - head, width + whole // 2), tile.dtype),
            jax.ShapeDtypeStruct((rows, width + whole // 2), tile.dtype),
        ],
        compiler_params=pltpu.CompilerParams(vmem_limit_bytes=LIMIT),
        cost_estimate=work(0, 4 * rows * (width + whole)),
        name="pack",
    )(
        pltpu.with_memory_space_constraint(tile, pltpu.HBM),
        pltpu.with_memory_space_constraint(grads, pltpu.HBM),
    )


def block_body(grad_starts, scale_start, step, carried, *refs):
    pieces, refs = refs[: len(grad_starts)], refs[len(grad_starts) :]
    scale_ref, *panels = refs[:5]
    carry_refs, refs = refs[5 : 5 + carried], refs[5 + carried :]
    hidden_ref, own_ref, other_ref, *part_refs = refs
    width, quarter = panels[0].shape
    rows = own_ref.shape[0]
    kept = hidden_ref.shape[0] - rows
    for carry_ref in carry_refs:
        hidden_ref[:kept, :] = carry_ref[pl.ds(carry_ref.shape[0] - kept, kept), :]
    values = joined(pieces, pl.ds(0, width))
    factor = scale_ref[pl.ds(scale_start, rows), :]
    grads = []
    for which, out_ref in enumerate((own_ref, other_ref)):
        gate_val = contract(values, panels[2 * which][...], 1, 0)
        up_val = contract(values, panels[2 * which + 1][...], 1, 0)
        columns = pl.ds(which * quarter, quarter)
        sigmoid_val = jax.nn.sigmoid(gate_val)
        activation = gate_val * sigmoid_val
        hidden_ref[kept:, columns] = b16(factor * activation * up_val)
        received = jnp.concatenate(
            [
                piece[:, pl.ds(start + which * quarter, quarter)]
                for piece, start in zip(pieces, grad_starts)
            ]
        )
        act_grad = factor * f32(received)
        up_grad = b16(act_grad * activation)
        gate_grad = b16(act_grad * up_val * sigmoid_val * (1.0 + gate_val * (1.0 - sigmoid_val)))
        out_ref[:, :quarter] = gate_grad
        out_ref[:, quarter:] = up_grad
        grads += [gate_grad.T, up_grad.T]
    for start in range(0, width, step):
        columns = pl.ds(start, step)
        part = b16(
            sum(contract(panel[columns, :], grad, 1, 0) for panel, grad in zip(panels, grads))
        ).T
        first = 0
        for part_ref in part_refs:
            part_ref[:, columns] = part[first : first + part_ref.shape[0]]
            first += part_ref.shape[0]


def block_pass(pieces, grad_starts, scales, scale_start, panels, part_rows, carry=()):
    rows = sum(piece.shape[0] for piece in pieces)
    width, quarter = panels[0].shape

    def wide(count):
        return jax.ShapeDtypeStruct((count, 2 * quarter), jnp.bfloat16)

    hidden, own, other, *parts = pl.pallas_call(
        functools.partial(block_body, grad_starts, scale_start, column_step(width), len(carry)),
        out_shape=[wide(rows + len(carry) * rows), wide(rows), wide(rows)]
        + [jax.ShapeDtypeStruct((count, width), jnp.bfloat16) for count in part_rows],
        compiler_params=pltpu.CompilerParams(vmem_limit_bytes=LIMIT),
        cost_estimate=work(16 * rows * width * quarter, 4 * rows * width),
        name="block_pass",
    )(*pieces, scales, *panels, *carry)
    return hidden, own, other, parts


def weight_body(piece_count, grad_count, step, *refs):
    pieces, refs = refs[:piece_count], refs[piece_count:]
    grad_refs, refs = refs[:grad_count], refs[grad_count:]
    *outs, held_ref, out_sems = refs
    got_ref, outs = (None, outs) if len(outs) == 1 else (outs[0], outs[1:])
    width, columns = outs[0].shape
    chunks = width // step
    grads = joined(grad_refs, slice(None))

    def store(chunk):
        slot = chunk % 2
        return [
            pltpu.make_async_copy(
                held_ref.at[slot, :, pl.ds(index * columns, columns)],
                out_ref.at[pl.ds(chunk * step, step), :],
                out_sems.at[slot, index],
            )
            for index, out_ref in enumerate(outs)
        ]

    for chunk in range(chunks):
        slot = chunk % 2
        total = contract(joined(pieces, pl.ds(chunk * step, step)), grads, 0, 0)
        if got_ref is not None:
            total = (total + f32(got_ref[pl.ds(chunk * step, step), :])) * (1.0 / TILE)
        if chunk >= 2:
            for copy in store(chunk - 2):
                copy.wait()
        held_ref[slot] = b16(total)
        for copy in store(chunk):
            copy.start()
    for chunk in range(max(chunks - 2, 0), chunks):
        for copy in store(chunk):
            copy.wait()


def weight_pass(width, pieces, grads, got=None):
    both = grads[0].shape[1]
    rows = sum(piece.shape[0] for piece in pieces)
    step = column_step(width)
    widths = [both] if got is None else [both // 2] * 2
    here, there = pl.BlockSpec(memory_space=pltpu.VMEM), pl.BlockSpec(memory_space=pl.ANY)
    return pl.pallas_call(
        functools.partial(weight_body, len(pieces), len(grads), step),
        in_specs=[here] * (len(pieces) + len(grads) + (got is not None)),
        out_specs=[there] * len(widths),
        out_shape=[jax.ShapeDtypeStruct((width, columns), jnp.bfloat16) for columns in widths],
        scratch_shapes=[
            pltpu.VMEM((2, step, both), jnp.bfloat16),
            pltpu.SemaphoreType.DMA((2, 2)),
        ],
        compiler_params=pltpu.CompilerParams(vmem_limit_bytes=LIMIT),
        cost_estimate=work(2 * rows * width * both, 2 * width * (rows + 2 * both)),
        name="weight_pass",
    )(
        *(
            pltpu.with_memory_space_constraint(part, pltpu.VMEM)
            for part in (*pieces, *grads, *([] if got is None else [got]))
        )
    )


def join_body(home_ref, far_ref, out_ref):
    kept = out_ref.shape[0] - far_ref.shape[0]
    out_ref[:kept, :] = home_ref[:kept, :]
    out_ref[kept:, :] = b16(f32(home_ref[kept:, :]) + f32(far_ref[...]))


def join(home, far):
    return pl.pallas_call(
        join_body,
        out_shape=jax.ShapeDtypeStruct(home.shape, home.dtype),
        compiler_params=pltpu.CompilerParams(vmem_limit_bytes=LIMIT),
        cost_estimate=LONG,
        name="join",
    )(home, far)


def final_body(
    near_ref,
    first_ref,
    low_near_ref,
    head_ref,
    low_ref,
    hidden_near_ref,
    hidden_far_ref,
    hidden_back_ref,
    hidden_got_ref,
    tokens_ref,
    hidden_ref,
):
    rows = tokens_ref.shape[0]
    first, head = first_ref.shape[0], head_ref.shape[0]
    rest = head - first
    tokens_ref[:first, :] = b16(
        f32(near_ref[:first, :]) + f32(first_ref[...]) + f32(head_ref[:first, :])
    )
    tokens_ref[first:head, :] = b16(
        f32(near_ref[first:head, :]) + f32(low_ref[:rest, :]) + f32(head_ref[first:, :])
    )
    tokens_ref[head:, :] = b16(
        f32(near_ref[head:, :]) + f32(low_near_ref[...]) + f32(low_ref[rest:, :])
    )
    rank = lax.axis_index("dp")
    quarter = hidden_ref.shape[2]
    for block, home_ref in enumerate((hidden_near_ref, hidden_far_ref)):
        back = hidden_back_ref[pl.ds(block * rows, rows), :quarter]
        hidden_ref[(2 * block) ^ rank] = b16(f32(home_ref[:rows, :quarter]) + f32(back))
        hidden_ref[(2 * block + 1) ^ rank] = hidden_got_ref[pl.ds(block * rows, rows), :]


def final(near, *others):
    rows = near.shape[0]
    quarter = others[-1].shape[1]
    return pl.pallas_call(
        final_body,
        out_shape=[
            jax.ShapeDtypeStruct(near.shape, near.dtype),
            jax.ShapeDtypeStruct((4, rows, quarter), near.dtype),
        ],
        compiler_params=pltpu.CompilerParams(vmem_limit_bytes=LIMIT),
        cost_estimate=LONG,
        name="final",
    )(*(pltpu.with_memory_space_constraint(part, pltpu.VMEM) for part in (near, *others)))


def per_device(tokens, cotangent, gate_weights, tile_expert, w_gate, w_up):
    row_count = tokens.shape[1]
    tile_count = row_count // TILE
    cycle_size = lax.axis_size("expert")
    position = lax.axis_index("expert")
    before = (position + cycle_size - 1) % cycle_size
    group_count = lax.axis_size("dp")
    rank = lax.axis_index("dp")
    quarter = w_gate.shape[2]
    out_head = OUT_SHARE * tile_count
    first, head = (share * tile_count for share in BACK_SHARE)
    tile, tile_grad = tokens[0], cotangent[0]

    def row_scale(group, place):
        owners = lax.dynamic_slice(tile_expert, (group, place * tile_count), (1, tile_count))
        weights = lax.dynamic_slice(gate_weights, (group, place * row_count), (1, row_count))
        routed = jnp.repeat(owners == position, TILE, axis=1, total_repeat_length=row_count)
        return jnp.where(routed, weights, jnp.zeros_like(weights)).reshape(row_count, 1)

    far = (rank + group_count // 2) % group_count
    scales = jnp.concatenate(
        [
            row_scale(group, place)
            for group, place in ((rank, position), (far, position), (rank, before), (far, before))
        ]
    )

    width = tile.shape[1]
    sent_at, kept_at = width, width + 2 * quarter
    near_top, near_low, far_message = pack(tile, tile_grad, out_head)
    x_top, x_low, y_tile = shifted(near_top, 1), shifted(near_low, 1), across(far_message)
    panels = (w_gate[0], w_up[0], within(w_gate[0]), within(w_up[0]))
    hid_hn, own_hn, other_hn, (part_hn,) = block_pass(
        (near_top, near_low), (kept_at, sent_at), scales, 0, panels, (row_count,)
    )
    x_top = after(x_top, hid_hn)
    x_sent = x_top[:, :kept_at]
    xy_top = across(x_sent)
    y_tile = after(y_tile, x_sent)
    y_sent = y_tile[out_head:]
    xy_low = shifted(y_sent, 1)
    x_low = after(x_low, y_sent)

    lower = row_count - head
    hid_mid, own_mid, other_mid, (first_hf, rest_hf, head_pn, lower_pn) = block_pass(
        (y_tile, x_top, x_low),
        (sent_at, kept_at, sent_at),
        scales,
        row_count,
        panels,
        (first, row_count - first, head, lower),
    )
    first_home = across(first_hf)
    low_near = shifted(lower_pn, -1)
    xy_low, xy_top = after((xy_low, xy_top), hid_mid)
    hid_past, own_pf, other_pf, (head_pf, lower_pf) = block_pass(
        (xy_top, xy_low), (sent_at, sent_at), scales, 3 * row_count, panels, (head, lower), (hid_mid,)
    )
    head_past = across(head_pf)
    low_far = shifted(lower_pf, -1)

    pieces = (near_top, near_low, y_tile, x_top, x_low, xy_top, xy_low)
    (sent,) = weight_pass(width, pieces, after((other_hn, other_mid, other_pf), first_home, low_near))
    got = within(sent)
    hid_back = shifted(after(hid_past, sent), -1)
    head_sum = b16(f32(head_pn) + f32(after(head_past, sent)))
    head_back = shifted(head_sum, -1)
    low_sum = join(rest_hf, after(low_far, head_sum))
    hid_back = after(hid_back, low_sum)
    low_home = across(low_sum)
    hid_other = jnp.concatenate([hid_hn[:, quarter:], hid_mid[:row_count, quarter:]])
    hid_other = b16(f32(hid_other) + f32(hid_back[:, quarter:]))
    hid_got = within(hid_other)
    got = after(got, hid_other, low_sum)
    grad_gate, grad_up = weight_pass(width, pieces, (own_hn, own_mid, own_pf), got)
    d_tokens, hidden = final(
        part_hn,
        *(first_home, low_near, head_back, low_home),
        *(hid_hn, hid_mid, hid_back, after(hid_got, grad_gate)),
    )
    return (d_tokens[None], hidden, grad_gate[None], grad_up[None])


def solution(mesh):
    in_specs = (
        P("dp", "expert", None),
        P("dp", "expert", None),
        P(),
        P(),
        P("expert", None, "dp"),
        P("expert", None, "dp"),
    )
    out_specs = (
        P("dp", "expert", None),
        P(None, "expert", "dp"),
        P("expert", None, "dp"),
        P("expert", None, "dp"),
    )
    return jax.shard_map(
        per_device, mesh=mesh, in_specs=in_specs, out_specs=out_specs, check_vma=False
    )
```

```python
import functools

import jax
import jax.numpy as jnp
from jax import lax
from jax.experimental import pallas as pl
from jax.experimental.pallas import tpu as pltpu
from jax.sharding import PartitionSpec as P

TILE = 128
OUT_SHARE = 80
BACK_SHARE = (48, 64)
LIMIT = 20 * 2**20
LONG = pl.CostEstimate(flops=10**12, bytes_accessed=10**9, transcendentals=0)


def work(flops, moved):
    return pl.CostEstimate(flops=flops, bytes_accessed=moved, transcendentals=0)


def shifted(value, steps):
    count = lax.axis_size("expert")
    pairs = [(source, (source + steps) % count) for source in range(count)]
    return lax.ppermute(value, "expert", pairs)


def across(value):
    count = lax.axis_size("dp")
    pairs = [(source, (source + count // 2) % count) for source in range(count)]
    return lax.ppermute(value, "dp", pairs)


def within(value):
    count = lax.axis_size("dp")
    pairs = [(source, source + 1 - 2 * (source % 2)) for source in range(count)]
    return lax.ppermute(value, "dp", pairs)


def after(values, *earlier):
    return lax.optimization_barrier((values, earlier))[0]


def f32(value):
    return value.astype(jnp.float32)


def b16(value):
    return value.astype(jnp.bfloat16)


def column_step(width):
    for step in (512, 256, 128):
        if width % step == 0:
            return step
    return width


def contract(left, right, left_axis, right_axis):
    return lax.dot_general(
        left, right, (((left_axis,), (right_axis,)), ((), ())), preferred_element_type=jnp.float32
    )


def joined(refs, columns):
    return jnp.concatenate([ref[:, columns] for ref in refs], axis=0)


def pack_body(tile_ref, grads_ref, top_ref, low_ref, sent_ref):
    rank = lax.axis_index("dp")
    side, core = rank // 2, rank % 2
    width = tile_ref.shape[1]
    quarter = grads_ref.shape[1] // 4
    head, both = top_ref.shape[0], 2 * quarter
    parts = [
        grads_ref[:, pl.ds(pl.multiple_of((2 * which + first) * quarter, quarter), quarter)]
        for which in (1 - side, side)
        for first in (core, 1 - core)
    ]
    sent, kept = jnp.concatenate(parts[:2], axis=1), jnp.concatenate(parts[2:], axis=1)
    sent_ref[...] = sent
    top_ref[:, :width] = tile_ref[:head, :]
    top_ref[:, width : width + both] = sent[:head]
    top_ref[:, width + both :] = kept[:head]
    low_ref[:, :width] = tile_ref[head:, :]
    low_ref[:, width:] = kept[head:]


def pack(tile, grads, head):
    rows, width = tile.shape
    whole = grads.shape[1]
    return pl.pallas_call(
        pack_body,
        out_shape=[
            jax.ShapeDtypeStruct((head, width + whole), tile.dtype),
            jax.ShapeDtypeStruct((rows - head, width + whole // 2), tile.dtype),
            jax.ShapeDtypeStruct((rows, whole // 2), tile.dtype),
        ],
        compiler_params=pltpu.CompilerParams(vmem_limit_bytes=LIMIT),
        cost_estimate=work(0, 4 * rows * (width + whole)),
        name="pack",
    )(
        pltpu.with_memory_space_constraint(tile, pltpu.HBM),
        pltpu.with_memory_space_constraint(grads, pltpu.HBM),
    )


def block_body(piece_count, sources, extra, scale_start, step, carried, handed, *refs):
    held, refs = refs[: piece_count + extra], refs[piece_count + extra :]
    pieces = held[:piece_count]
    scale_ref, *panels = refs[:5]
    carry_refs, refs = refs[5 : 5 + carried], refs[5 + carried :]
    hidden_ref, own_ref, other_ref, *part_refs = refs
    for index, panel_index in enumerate(handed):
        part_refs[index][...] = panels[panel_index][...]
    part_refs = part_refs[len(handed) :]
    width, quarter = panels[0].shape
    rows = own_ref.shape[0]
    kept = hidden_ref.shape[0] - rows
    for carry_ref in carry_refs:
        hidden_ref[:kept, :] = carry_ref[pl.ds(carry_ref.shape[0] - kept, kept), :]
    values = joined(pieces, pl.ds(0, width))
    factor = scale_ref[pl.ds(scale_start, rows), :]
    grads = []
    for which, out_ref in enumerate((own_ref, other_ref)):
        gate_val = contract(values, panels[2 * which][...], 1, 0)
        up_val = contract(values, panels[2 * which + 1][...], 1, 0)
        columns = pl.ds(which * quarter, quarter)
        sigmoid_val = jax.nn.sigmoid(gate_val)
        activation = gate_val * sigmoid_val
        hidden_ref[kept:, columns] = b16(factor * activation * up_val)
        received = jnp.concatenate(
            [
                held[index][:, pl.ds(start + which * quarter, quarter)]
                for index, start in sources
            ]
        )
        act_grad = factor * f32(received)
        up_grad = b16(act_grad * activation)
        gate_grad = b16(act_grad * up_val * sigmoid_val * (1.0 + gate_val * (1.0 - sigmoid_val)))
        out_ref[:, :quarter] = gate_grad
        out_ref[:, quarter:] = up_grad
        grads += [gate_grad.T, up_grad.T]
    for start in range(0, width, step):
        columns = pl.ds(start, step)
        part = b16(
            sum(contract(panel[columns, :], grad, 1, 0) for panel, grad in zip(panels, grads))
        ).T
        first = 0
        for part_ref in part_refs:
            part_ref[:, columns] = part[first : first + part_ref.shape[0]]
            first += part_ref.shape[0]


def block_pass(
    pieces, sources, scales, scale_start, panels, part_rows, extra=(), carry=(), handed=()
):
    rows = sum(piece.shape[0] for piece in pieces)
    width, quarter = panels[0].shape

    def wide(count):
        return jax.ShapeDtypeStruct((count, 2 * quarter), jnp.bfloat16)

    hidden, own, other, *parts = pl.pallas_call(
        functools.partial(
            block_body,
            len(pieces),
            sources,
            len(extra),
            scale_start,
            column_step(width),
            len(carry),
            handed,
        ),
        out_shape=[wide(rows + len(carry) * rows), wide(rows), wide(rows)]
        + [jax.ShapeDtypeStruct((width, quarter), jnp.bfloat16)] * len(handed)
        + [jax.ShapeDtypeStruct((count, width), jnp.bfloat16) for count in part_rows],
        compiler_params=pltpu.CompilerParams(vmem_limit_bytes=LIMIT),
        cost_estimate=work(16 * rows * width * quarter, 4 * rows * width),
        name="block_pass",
    )(*pieces, *extra, scales, *panels, *carry)
    return hidden, own, other, parts


def weight_body(piece_count, grad_count, step, *refs):
    pieces, refs = refs[:piece_count], refs[piece_count:]
    grad_refs, refs = refs[:grad_count], refs[grad_count:]
    *outs, held_ref, got_held_ref, out_sems, got_sems = refs
    got_ref, outs = (None, outs) if len(outs) == 1 else (outs[0], outs[1:])
    width, columns = outs[0].shape
    chunks = width // step
    grads = joined(grad_refs, slice(None))

    def fetch(chunk):
        rows = pl.ds(chunk * step, step)
        return pltpu.make_async_copy(got_ref.at[rows, :], got_held_ref.at[rows, :], got_sems.at[chunk])

    def store(chunk):
        slot = chunk % 2
        return [
            pltpu.make_async_copy(
                held_ref.at[slot, :, pl.ds(index * columns, columns)],
                out_ref.at[pl.ds(chunk * step, step), :],
                out_sems.at[slot, index],
            )
            for index, out_ref in enumerate(outs)
        ]

    if got_ref is not None:
        for chunk in range(chunks):
            fetch(chunk).start()
    for chunk in range(chunks):
        slot = chunk % 2
        total = contract(joined(pieces, pl.ds(chunk * step, step)), grads, 0, 0)
        if got_ref is not None:
            fetch(chunk).wait()
            total = (total + f32(got_held_ref[pl.ds(chunk * step, step), :])) * (1.0 / TILE)
        if chunk >= 2:
            for copy in store(chunk - 2):
                copy.wait()
        held_ref[slot] = b16(total)
        for copy in store(chunk):
            copy.start()
    for chunk in range(max(chunks - 2, 0), chunks):
        for copy in store(chunk):
            copy.wait()


def weight_pass(width, pieces, grads, got=None):
    both = grads[0].shape[1]
    rows = sum(piece.shape[0] for piece in pieces)
    step = column_step(width)
    widths = [both] if got is None else [both // 2] * 2
    here, there = pl.BlockSpec(memory_space=pltpu.VMEM), pl.BlockSpec(memory_space=pl.ANY)
    return pl.pallas_call(
        functools.partial(weight_body, len(pieces), len(grads), step),
        in_specs=[here] * (len(pieces) + len(grads)) + ([] if got is None else [there]),
        out_specs=[there] * len(widths),
        out_shape=[jax.ShapeDtypeStruct((width, columns), jnp.bfloat16) for columns in widths],
        scratch_shapes=[
            pltpu.VMEM((2, step, both), jnp.bfloat16),
            pltpu.VMEM((step if got is None else width, both), jnp.bfloat16),
            pltpu.SemaphoreType.DMA((2, 2)),
            pltpu.SemaphoreType.DMA((width // step,)),
        ],
        compiler_params=pltpu.CompilerParams(vmem_limit_bytes=LIMIT),
        cost_estimate=work(2 * rows * width * both, 2 * width * (rows + 2 * both)),
        name="weight_pass",
    )(
        *(pltpu.with_memory_space_constraint(part, pltpu.VMEM) for part in (*pieces, *grads)),
        *([] if got is None else [got]),
    )


def join_body(home_ref, far_ref, out_ref):
    kept = out_ref.shape[0] - far_ref.shape[0]
    if kept:
        out_ref[:kept, :] = home_ref[:kept, :]
    out_ref[kept:, :] = b16(f32(home_ref[kept:, :]) + f32(far_ref[...]))


def join(home, far, cost):
    return pl.pallas_call(
        join_body,
        out_shape=jax.ShapeDtypeStruct(home.shape, home.dtype),
        compiler_params=pltpu.CompilerParams(vmem_limit_bytes=LIMIT),
        cost_estimate=cost,
        name="join",
    )(home, far)


def final_body(
    near_ref,
    first_ref,
    low_near_ref,
    head_ref,
    low_ref,
    hidden_near_ref,
    hidden_far_ref,
    hidden_back_ref,
    hidden_got_ref,
    tokens_ref,
    hidden_ref,
):
    rows = tokens_ref.shape[0]
    first, head = first_ref.shape[0], head_ref.shape[0]
    rest = head - first
    tokens_ref[:first, :] = b16(
        f32(near_ref[:first, :]) + f32(first_ref[...]) + f32(head_ref[:first, :])
    )
    tokens_ref[first:head, :] = b16(
        f32(near_ref[first:head, :]) + f32(low_ref[:rest, :]) + f32(head_ref[first:, :])
    )
    tokens_ref[head:, :] = b16(
        f32(near_ref[head:, :]) + f32(low_near_ref[...]) + f32(low_ref[rest:, :])
    )
    rank = lax.axis_index("dp")
    quarter = hidden_ref.shape[2]
    for block, home_ref in enumerate((hidden_near_ref, hidden_far_ref)):
        back = hidden_back_ref[pl.ds(block * rows, rows), :quarter]
        hidden_ref[(2 * block) ^ rank] = b16(f32(home_ref[:rows, :quarter]) + f32(back))
        hidden_ref[(2 * block + 1) ^ rank] = hidden_got_ref[pl.ds(block * rows, rows), :]


def final(near, *others):
    rows = near.shape[0]
    quarter = others[-1].shape[1]
    return pl.pallas_call(
        final_body,
        out_shape=[
            jax.ShapeDtypeStruct(near.shape, near.dtype),
            jax.ShapeDtypeStruct((4, rows, quarter), near.dtype),
        ],
        compiler_params=pltpu.CompilerParams(vmem_limit_bytes=LIMIT),
        cost_estimate=LONG,
        name="final",
    )(*(pltpu.with_memory_space_constraint(part, pltpu.VMEM) for part in (near, *others)))


def per_device(tokens, cotangent, gate_weights, tile_expert, w_gate, w_up):
    row_count = tokens.shape[1]
    tile_count = row_count // TILE
    cycle_size = lax.axis_size("expert")
    position = lax.axis_index("expert")
    before = (position + cycle_size - 1) % cycle_size
    group_count = lax.axis_size("dp")
    rank = lax.axis_index("dp")
    quarter = w_gate.shape[2]
    out_head = OUT_SHARE * tile_count
    first, head = (share * tile_count for share in BACK_SHARE)
    tile, tile_grad = tokens[0], cotangent[0]

    def row_scale(group, place):
        owners = lax.dynamic_slice(tile_expert, (group, place * tile_count), (1, tile_count))
        weights = lax.dynamic_slice(gate_weights, (group, place * row_count), (1, row_count))
        routed = jnp.repeat(owners == position, TILE, axis=1, total_repeat_length=row_count)
        return jnp.where(routed, weights, jnp.zeros_like(weights)).reshape(row_count, 1)

    far = (rank + group_count // 2) % group_count
    scales = jnp.concatenate(
        [
            row_scale(group, place)
            for group, place in ((rank, position), (far, position), (rank, before), (far, before))
        ]
    )

    width = tile.shape[1]
    sent_at, kept_at = width, width + 2 * quarter
    y_tile = across(tile)
    near_top, near_low, near_sent = pack(tile, tile_grad, out_head)
    x_top, x_low, y_grads = shifted(near_top, 1), shifted(near_low, 1), across(near_sent)
    panels = (w_gate[0], w_up[0], within(w_gate[0]), within(w_up[0]))
    hid_hn, own_hn, other_hn, (part_hn,) = block_pass(
        (near_top, near_low), ((0, kept_at), (1, sent_at)), scales, 0, panels, (row_count,)
    )
    x_top, y_grads = after((x_top, y_grads), hid_hn)
    x_sent = x_top[:, :kept_at]
    xy_top = across(x_sent)
    y_tile = after(y_tile, x_sent)
    y_sent = jnp.concatenate([y_tile[out_head:], y_grads[out_head:]], axis=1)
    xy_low = shifted(y_sent, 1)
    x_low = after(x_low, y_sent)

    lower = row_count - head
    hid_mid, own_mid, other_mid, mid_parts = block_pass(
        (y_tile, x_top, x_low),
        ((3, 0), (1, kept_at), (2, sent_at)),
        scales,
        row_count,
        panels,
        (first, row_count - first, head, lower),
        extra=(y_grads,),
        handed=(2, 3),
    )
    *handed, first_hf, rest_hf, head_pn, lower_pn = mid_parts
    first_home = across(first_hf)
    low_near = shifted(lower_pn, -1)
    xy_low, xy_top = after((xy_low, xy_top), hid_mid)
    hid_past, own_pf, other_pf, (head_pf, lower_pf) = block_pass(
        (xy_top, xy_low),
        ((0, sent_at), (1, sent_at)),
        scales,
        3 * row_count,
        (*panels[:2], *handed),
        (head, lower),
        carry=(hid_mid,),
    )
    head_past = across(head_pf)
    low_far = shifted(lower_pf, -1)

    pieces = (near_top, near_low, y_tile, x_top, x_low, xy_top, xy_low)
    (sent,) = weight_pass(width, pieces, after((other_hn, other_mid, other_pf), first_home, low_near))
    got = within(sent)
    hid_back = shifted(after(hid_past, sent), -1)
    head_sum = join(head_pn, after(head_past, sent), work(0, 0))
    head_back = shifted(head_sum, -1)
    low_sum = join(rest_hf, after(low_far, head_sum), LONG)
    low_home = across(low_sum)
    got = after(got, low_sum)
    grad_gate, grad_up = weight_pass(width, pieces, (own_hn, own_mid, own_pf), got)
    hid_back = after(hid_back, grad_gate)
    hid_other = jnp.concatenate([hid_hn[:, quarter:], hid_mid[:row_count, quarter:]])
    hid_other = b16(f32(hid_other) + f32(hid_back[:, quarter:]))
    hid_got = within(hid_other)
    d_tokens, hidden = final(
        part_hn,
        *(first_home, low_near, head_back, low_home),
        *(hid_hn, hid_mid, hid_back, hid_got),
    )
    return (d_tokens[None], hidden, grad_gate[None], grad_up[None])


def solution(mesh):
    in_specs = (
        P("dp", "expert", None),
        P("dp", "expert", None),
        P(),
        P(),
        P("expert", None, "dp"),
        P("expert", None, "dp"),
    )
    out_specs = (
        P("dp", "expert", None),
        P(None, "expert", "dp"),
        P("expert", None, "dp"),
        P("expert", None, "dp"),
    )
    return jax.shard_map(
        per_device, mesh=mesh, in_specs=in_specs, out_specs=out_specs, check_vma=False
    )
```

```python
import functools

import jax
import jax.numpy as jnp
from jax import lax
from jax.experimental import pallas as pl
from jax.experimental.pallas import tpu as pltpu
from jax.sharding import PartitionSpec as P

TILE = 128
OUT_SHARE = 80
BACK_SHARE = (48, 64)
LIMIT = 20 * 2**20
LONG = pl.CostEstimate(flops=10**12, bytes_accessed=10**9, transcendentals=0)


def work(flops, moved):
    return pl.CostEstimate(flops=flops, bytes_accessed=moved, transcendentals=0)


def shifted(value, steps):
    count = lax.axis_size("expert")
    pairs = [(source, (source + steps) % count) for source in range(count)]
    return lax.ppermute(value, "expert", pairs)


def across(value):
    count = lax.axis_size("dp")
    pairs = [(source, (source + count // 2) % count) for source in range(count)]
    return lax.ppermute(value, "dp", pairs)


def within(value):
    count = lax.axis_size("dp")
    pairs = [(source, source + 1 - 2 * (source % 2)) for source in range(count)]
    return lax.ppermute(value, "dp", pairs)


def after(values, *earlier):
    return lax.optimization_barrier((values, earlier))[0]


def f32(value):
    return value.astype(jnp.float32)


def b16(value):
    return value.astype(jnp.bfloat16)


def column_step(width):
    for step in (512, 256, 128):
        if width % step == 0:
            return step
    return width


def contract(left, right, left_axis, right_axis):
    return lax.dot_general(
        left, right, (((left_axis,), (right_axis,)), ((), ())), preferred_element_type=jnp.float32
    )


def joined(refs, columns):
    return jnp.concatenate([ref[:, columns] for ref in refs], axis=0)


def pack_body(tile_ref, grads_ref, top_ref, low_ref, sent_ref):
    rank = lax.axis_index("dp")
    side, core = rank // 2, rank % 2
    width = tile_ref.shape[1]
    quarter = grads_ref.shape[1] // 4
    head = top_ref.shape[0]
    parts = [
        grads_ref[:, pl.ds(pl.multiple_of((2 * which + first) * quarter, quarter), quarter)]
        for which in (1 - side, side)
        for first in (core, 1 - core)
    ]
    sent, kept = jnp.concatenate(parts[:2], axis=1), jnp.concatenate(parts[2:], axis=1)
    sent_ref[...] = sent
    top_ref[:, :width] = tile_ref[:head, :]
    top_ref[:, width:] = kept[:head]
    low_ref[:, :width] = tile_ref[head:, :]
    low_ref[:, width:] = kept[head:]


def pack(tile, grads, head):
    rows, width = tile.shape
    whole = grads.shape[1]
    return pl.pallas_call(
        pack_body,
        out_shape=[
            jax.ShapeDtypeStruct((head, width + whole // 2), tile.dtype),
            jax.ShapeDtypeStruct((rows - head, width + whole // 2), tile.dtype),
            jax.ShapeDtypeStruct((rows, whole // 2), tile.dtype),
        ],
        compiler_params=pltpu.CompilerParams(vmem_limit_bytes=LIMIT),
        cost_estimate=work(0, 4 * rows * (width + whole)),
        name="pack",
    )(
        pltpu.with_memory_space_constraint(tile, pltpu.HBM),
        pltpu.with_memory_space_constraint(grads, pltpu.HBM),
    )


def block_body(piece_count, sources, extra, scale_start, step, carried, handed, *refs):
    held, refs = refs[: piece_count + extra], refs[piece_count + extra :]
    pieces = held[:piece_count]
    scale_ref, *panels = refs[:5]
    carry_refs, refs = refs[5 : 5 + carried], refs[5 + carried :]
    hidden_ref, own_ref, other_ref, *part_refs = refs
    for index, panel_index in enumerate(handed):
        part_refs[index][...] = panels[panel_index][...]
    part_refs = part_refs[len(handed) :]
    width, quarter = panels[0].shape
    rows = own_ref.shape[0]
    kept = hidden_ref.shape[0] - rows
    for carry_ref in carry_refs:
        hidden_ref[:kept, :] = carry_ref[pl.ds(carry_ref.shape[0] - kept, kept), :]
    values = joined(pieces, pl.ds(0, width))
    factor = scale_ref[pl.ds(scale_start, rows), :]
    grads = []
    for which, out_ref in enumerate((own_ref, other_ref)):
        gate_val = contract(values, panels[2 * which][...], 1, 0)
        up_val = contract(values, panels[2 * which + 1][...], 1, 0)
        columns = pl.ds(which * quarter, quarter)
        sigmoid_val = jax.nn.sigmoid(gate_val)
        activation = gate_val * sigmoid_val
        hidden_ref[kept:, columns] = b16(factor * activation * up_val)
        received = jnp.concatenate(
            [
                held[index][:, pl.ds(start + which * quarter, quarter)]
                for index, start in sources
            ]
        )
        act_grad = factor * f32(received)
        up_grad = b16(act_grad * activation)
        gate_grad = b16(act_grad * up_val * sigmoid_val * (1.0 + gate_val * (1.0 - sigmoid_val)))
        out_ref[:, :quarter] = gate_grad
        out_ref[:, quarter:] = up_grad
        grads += [gate_grad.T, up_grad.T]
    for start in range(0, width, step):
        columns = pl.ds(start, step)
        part = b16(
            sum(contract(panel[columns, :], grad, 1, 0) for panel, grad in zip(panels, grads))
        ).T
        first = 0
        for part_ref in part_refs:
            part_ref[:, columns] = part[first : first + part_ref.shape[0]]
            first += part_ref.shape[0]


def block_pass(
    pieces, sources, scales, scale_start, panels, part_rows, extra=(), carry=(), handed=()
):
    rows = sum(piece.shape[0] for piece in pieces)
    width, quarter = panels[0].shape

    def wide(count):
        return jax.ShapeDtypeStruct((count, 2 * quarter), jnp.bfloat16)

    hidden, own, other, *parts = pl.pallas_call(
        functools.partial(
            block_body,
            len(pieces),
            sources,
            len(extra),
            scale_start,
            column_step(width),
            len(carry),
            handed,
        ),
        out_shape=[wide(rows + len(carry) * rows), wide(rows), wide(rows)]
        + [jax.ShapeDtypeStruct((width, quarter), jnp.bfloat16)] * len(handed)
        + [jax.ShapeDtypeStruct((count, width), jnp.bfloat16) for count in part_rows],
        compiler_params=pltpu.CompilerParams(vmem_limit_bytes=LIMIT),
        cost_estimate=work(16 * rows * width * quarter, 4 * rows * width),
        name="block_pass",
    )(*pieces, *extra, scales, *panels, *carry)
    return hidden, own, other, parts


def weight_body(piece_count, grad_count, step, *refs):
    pieces, refs = refs[:piece_count], refs[piece_count:]
    grad_refs, refs = refs[:grad_count], refs[grad_count:]
    *outs, held_ref, got_held_ref, out_sems, got_sems = refs
    got_ref, outs = (None, outs) if len(outs) == 1 else (outs[0], outs[1:])
    width, columns = outs[0].shape
    chunks = width // step
    grads = joined(grad_refs, slice(None))

    def fetch(chunk):
        rows = pl.ds(chunk * step, step)
        return pltpu.make_async_copy(got_ref.at[rows, :], got_held_ref.at[rows, :], got_sems.at[chunk])

    def store(chunk):
        slot = chunk % 2
        return [
            pltpu.make_async_copy(
                held_ref.at[slot, :, pl.ds(index * columns, columns)],
                out_ref.at[pl.ds(chunk * step, step), :],
                out_sems.at[slot, index],
            )
            for index, out_ref in enumerate(outs)
        ]

    if got_ref is not None:
        for chunk in range(chunks):
            fetch(chunk).start()
    for chunk in range(chunks):
        slot = chunk % 2
        total = contract(joined(pieces, pl.ds(chunk * step, step)), grads, 0, 0)
        if got_ref is not None:
            fetch(chunk).wait()
            total = (total + f32(got_held_ref[pl.ds(chunk * step, step), :])) * (1.0 / TILE)
        if chunk >= 2:
            for copy in store(chunk - 2):
                copy.wait()
        held_ref[slot] = b16(total)
        for copy in store(chunk):
            copy.start()
    for chunk in range(max(chunks - 2, 0), chunks):
        for copy in store(chunk):
            copy.wait()


def weight_pass(width, pieces, grads, got=None):
    both = grads[0].shape[1]
    rows = sum(piece.shape[0] for piece in pieces)
    step = column_step(width)
    widths = [both] if got is None else [both // 2] * 2
    here, there = pl.BlockSpec(memory_space=pltpu.VMEM), pl.BlockSpec(memory_space=pl.ANY)
    return pl.pallas_call(
        functools.partial(weight_body, len(pieces), len(grads), step),
        in_specs=[here] * (len(pieces) + len(grads)) + ([] if got is None else [there]),
        out_specs=[there] * len(widths),
        out_shape=[jax.ShapeDtypeStruct((width, columns), jnp.bfloat16) for columns in widths],
        scratch_shapes=[
            pltpu.VMEM((2, step, both), jnp.bfloat16),
            pltpu.VMEM((step if got is None else width, both), jnp.bfloat16),
            pltpu.SemaphoreType.DMA((2, 2)),
            pltpu.SemaphoreType.DMA((width // step,)),
        ],
        compiler_params=pltpu.CompilerParams(vmem_limit_bytes=LIMIT),
        cost_estimate=work(2 * rows * width * both, 2 * width * (rows + 2 * both)),
        name="weight_pass",
    )(
        *(pltpu.with_memory_space_constraint(part, pltpu.VMEM) for part in (*pieces, *grads)),
        *([] if got is None else [got]),
    )


def join_body(home_ref, far_ref, out_ref):
    kept = out_ref.shape[0] - far_ref.shape[0]
    if kept:
        out_ref[:kept, :] = home_ref[:kept, :]
    out_ref[kept:, :] = b16(f32(home_ref[kept:, :]) + f32(far_ref[...]))


def join(home, far, cost):
    return pl.pallas_call(
        join_body,
        out_shape=jax.ShapeDtypeStruct(home.shape, home.dtype),
        compiler_params=pltpu.CompilerParams(vmem_limit_bytes=LIMIT),
        cost_estimate=cost,
        name="join",
    )(home, far)


def final_body(
    near_ref,
    first_ref,
    low_near_ref,
    head_ref,
    low_ref,
    tokens_ref,
):
    rows = tokens_ref.shape[0]
    first, head = first_ref.shape[0], head_ref.shape[0]
    rest = head - first
    tokens_ref[:first, :] = b16(
        f32(near_ref[:first, :]) + f32(first_ref[...]) + f32(head_ref[:first, :])
    )
    tokens_ref[first:head, :] = b16(
        f32(near_ref[first:head, :]) + f32(low_ref[:rest, :]) + f32(head_ref[first:, :])
    )
    tokens_ref[head:, :] = b16(
        f32(near_ref[head:, :]) + f32(low_near_ref[...]) + f32(low_ref[rest:, :])
    )


def final(near, *others):
    return pl.pallas_call(
        final_body,
        out_shape=jax.ShapeDtypeStruct(near.shape, near.dtype),
        compiler_params=pltpu.CompilerParams(vmem_limit_bytes=LIMIT),
        cost_estimate=LONG,
        name="final",
    )(near, *others)


def hidden_body(near_ref, far_ref, back_ref, got_ref, out_ref):
    rank = lax.axis_index("dp")
    _, rows, quarter = out_ref.shape
    for block, home_ref in enumerate((near_ref, far_ref)):
        part = pl.ds(block * rows, rows)
        home, back = home_ref[:rows, :quarter], back_ref[part, :quarter]
        out_ref[(2 * block) ^ rank] = b16(f32(home) + f32(back))
        out_ref[(2 * block + 1) ^ rank] = got_ref[part, :]


def hidden_pass(near, far, back, got):
    rows, both = near.shape
    return pl.pallas_call(
        hidden_body,
        out_shape=jax.ShapeDtypeStruct((4, rows, both // 2), near.dtype),
        compiler_params=pltpu.CompilerParams(vmem_limit_bytes=LIMIT),
        cost_estimate=work(0, 0),
        name="hidden_pass",
    )(near, far, back, got)


def per_device(tokens, cotangent, gate_weights, tile_expert, w_gate, w_up):
    row_count = tokens.shape[1]
    tile_count = row_count // TILE
    cycle_size = lax.axis_size("expert")
    position = lax.axis_index("expert")
    before = (position + cycle_size - 1) % cycle_size
    group_count = lax.axis_size("dp")
    rank = lax.axis_index("dp")
    quarter = w_gate.shape[2]
    out_head = OUT_SHARE * tile_count
    first, head = (share * tile_count for share in BACK_SHARE)
    tile, tile_grad = tokens[0], cotangent[0]

    def row_scale(group, place):
        owners = lax.dynamic_slice(tile_expert, (group, place * tile_count), (1, tile_count))
        weights = lax.dynamic_slice(gate_weights, (group, place * row_count), (1, row_count))
        routed = jnp.repeat(owners == position, TILE, axis=1, total_repeat_length=row_count)
        return jnp.where(routed, weights, jnp.zeros_like(weights)).reshape(row_count, 1)

    far = (rank + group_count // 2) % group_count
    scales = jnp.concatenate(
        [
            row_scale(group, place)
            for group, place in ((rank, position), (far, position), (rank, before), (far, before))
        ]
    )

    width = tile.shape[1]
    y_tile = across(tile)
    near_top, near_low, near_sent = pack(tile, tile_grad, out_head)
    x_top, x_low, y_grads = shifted(near_top, 1), shifted(near_low, 1), across(near_sent)
    panels = (w_gate[0], w_up[0], within(w_gate[0]), within(w_up[0]))
    hid_hn, own_hn, other_hn, (part_hn,) = block_pass(
        (near_top, near_low), ((0, width), (1, width)), scales, 0, panels, (row_count,)
    )
    x_top, y_grads = after((x_top, y_grads), hid_hn)
    x_sent = x_top[:, :width]
    xy_top = across(x_sent)
    y_tile = after(y_tile, x_sent)
    y_sent = y_tile[out_head:]
    xy_low = shifted(y_sent, 1)
    xy_grads = shifted(y_grads, 1)
    x_low = after(x_low, y_sent)

    lower = row_count - head
    hid_mid, own_mid, other_mid, mid_parts = block_pass(
        (y_tile, x_top, x_low),
        ((3, 0), (1, width), (2, width)),
        scales,
        row_count,
        panels,
        (first, row_count - first, head, lower),
        extra=(y_grads,),
        handed=(2, 3),
    )
    *handed, first_hf, rest_hf, head_pn, lower_pn = mid_parts
    first_home = across(first_hf)
    low_near = shifted(lower_pn, -1)
    xy_low, xy_top, xy_grads = after((xy_low, xy_top, xy_grads), hid_mid)
    hid_past, own_pf, other_pf, (head_pf, lower_pf) = block_pass(
        (xy_top, xy_low),
        ((2, 0),),
        scales,
        3 * row_count,
        (*panels[:2], *handed),
        (head, lower),
        extra=(xy_grads,),
        carry=(hid_mid,),
    )
    head_past = across(head_pf)
    low_far = shifted(lower_pf, -1)

    pieces = (near_top, near_low, y_tile, x_top, x_low, xy_top, xy_low)
    (sent,) = weight_pass(width, pieces, after((other_hn, other_mid, other_pf), first_home, low_near))
    got = within(sent)
    hid_back = shifted(after(hid_past, sent), -1)
    head_sum = join(head_pn, after(head_past, sent), work(0, 0))
    head_back = shifted(head_sum, -1)
    low_sum = join(rest_hf, after(low_far, head_sum), LONG)
    low_home = across(low_sum)
    got = after(got, low_sum)
    grad_gate, grad_up = weight_pass(width, pieces, (own_hn, own_mid, own_pf), got)
    hid_back = after(hid_back, grad_gate)
    hid_other = jnp.concatenate([hid_hn[:, quarter:], hid_mid[:row_count, quarter:]])
    hid_other = b16(f32(hid_other) + f32(hid_back[:, quarter:]))
    hid_got = within(hid_other)
    hidden = hidden_pass(hid_hn, hid_mid, hid_back, hid_got)
    d_tokens = final(part_hn, first_home, low_near, after(head_back, hidden), low_home)
    return (d_tokens[None], hidden, grad_gate[None], grad_up[None])


def solution(mesh):
    in_specs = (
        P("dp", "expert", None),
        P("dp", "expert", None),
        P(),
        P(),
        P("expert", None, "dp"),
        P("expert", None, "dp"),
    )
    out_specs = (
        P("dp", "expert", None),
        P(None, "expert", "dp"),
        P("expert", None, "dp"),
        P("expert", None, "dp"),
    )
    return jax.shard_map(
        per_device, mesh=mesh, in_specs=in_specs, out_specs=out_specs, check_vma=False
    )
```

```python
import functools

import jax
import jax.numpy as jnp
from jax import lax
from jax.experimental import pallas as pl
from jax.experimental.pallas import tpu as pltpu
from jax.sharding import PartitionSpec as P

TILE = 128
OUT_SHARE = 80
BACK_SHARE = (48, 80)
LIMIT = 20 * 2**20
LONG = pl.CostEstimate(flops=4 * 10**10, bytes_accessed=10**8, transcendentals=0)


def work(flops, moved):
    return pl.CostEstimate(flops=flops, bytes_accessed=moved, transcendentals=0)


def shifted(value, steps):
    count = lax.axis_size("expert")
    pairs = [(source, (source + steps) % count) for source in range(count)]
    return lax.ppermute(value, "expert", pairs)


def across(value):
    count = lax.axis_size("dp")
    pairs = [(source, (source + count // 2) % count) for source in range(count)]
    return lax.ppermute(value, "dp", pairs)


def within(value):
    count = lax.axis_size("dp")
    pairs = [(source, source + 1 - 2 * (source % 2)) for source in range(count)]
    return lax.ppermute(value, "dp", pairs)


def after(values, *earlier):
    return lax.optimization_barrier((values, earlier))[0]


def f32(value):
    return value.astype(jnp.float32)


def b16(value):
    return value.astype(jnp.bfloat16)


def column_step(width):
    for step in (512, 256, 128):
        if width % step == 0:
            return step
    return width


def contract(left, right, left_axis, right_axis):
    return lax.dot_general(
        left, right, (((left_axis,), (right_axis,)), ((), ())), preferred_element_type=jnp.float32
    )


def joined(refs, columns):
    return jnp.concatenate([ref[:, columns] for ref in refs], axis=0)


def pack_body(tile_ref, grads_ref, top_ref, low_ref, sent_ref):
    rank = lax.axis_index("dp")
    side, core = rank // 2, rank % 2
    width = tile_ref.shape[1]
    quarter = grads_ref.shape[1] // 4
    head = top_ref.shape[0]
    parts = [
        grads_ref[:, pl.ds(pl.multiple_of((2 * which + first) * quarter, quarter), quarter)]
        for which in (1 - side, side)
        for first in (core, 1 - core)
    ]
    sent, kept = jnp.concatenate(parts[:2], axis=1), jnp.concatenate(parts[2:], axis=1)
    sent_ref[...] = sent
    top_ref[:, :width] = tile_ref[:head, :]
    top_ref[:, width:] = kept[:head]
    low_ref[:, :width] = tile_ref[head:, :]
    low_ref[:, width:] = kept[head:]


def pack(tile, grads, head):
    rows, width = tile.shape
    whole = grads.shape[1]
    return pl.pallas_call(
        pack_body,
        out_shape=[
            jax.ShapeDtypeStruct((head, width + whole // 2), tile.dtype),
            jax.ShapeDtypeStruct((rows - head, width + whole // 2), tile.dtype),
            jax.ShapeDtypeStruct((rows, whole // 2), tile.dtype),
        ],
        compiler_params=pltpu.CompilerParams(vmem_limit_bytes=LIMIT),
        cost_estimate=work(0, 4 * rows * (width + whole)),
        name="pack",
    )(
        pltpu.with_memory_space_constraint(tile, pltpu.HBM),
        pltpu.with_memory_space_constraint(grads, pltpu.HBM),
    )


def block_body(piece_count, sources, extra, scale_start, step, carried, handed, *refs):
    held, refs = refs[: piece_count + extra], refs[piece_count + extra :]
    pieces = held[:piece_count]
    scale_ref, *panels = refs[:5]
    carry_refs, refs = refs[5 : 5 + carried], refs[5 + carried :]
    hidden_ref, own_ref, other_ref, *part_refs = refs
    for index, panel_index in enumerate(handed):
        part_refs[index][...] = panels[panel_index][...]
    part_refs = part_refs[len(handed) :]
    width, quarter = panels[0].shape
    rows = own_ref.shape[0]
    kept = hidden_ref.shape[0] - rows
    for carry_ref in carry_refs:
        hidden_ref[:kept, :] = carry_ref[pl.ds(carry_ref.shape[0] - kept, kept), :]
    values = joined(pieces, pl.ds(0, width))
    factor = scale_ref[pl.ds(scale_start, rows), :]
    grads = []
    for which, out_ref in enumerate((own_ref, other_ref)):
        gate_val = contract(values, panels[2 * which][...], 1, 0)
        up_val = contract(values, panels[2 * which + 1][...], 1, 0)
        columns = pl.ds(which * quarter, quarter)
        sigmoid_val = jax.nn.sigmoid(gate_val)
        activation = gate_val * sigmoid_val
        hidden_ref[kept:, columns] = b16(factor * activation * up_val)
        received = jnp.concatenate(
            [
                held[index][:, pl.ds(start + which * quarter, quarter)]
                for index, start in sources
            ]
        )
        act_grad = factor * f32(received)
        up_grad = b16(act_grad * activation)
        gate_grad = b16(act_grad * up_val * sigmoid_val * (1.0 + gate_val * (1.0 - sigmoid_val)))
        out_ref[:, :quarter] = gate_grad
        out_ref[:, quarter:] = up_grad
        grads += [gate_grad.T, up_grad.T]
    for start in range(0, width, step):
        columns = pl.ds(start, step)
        part = b16(
            sum(contract(panel[columns, :], grad, 1, 0) for panel, grad in zip(panels, grads))
        ).T
        first = 0
        for part_ref in part_refs:
            part_ref[:, columns] = part[first : first + part_ref.shape[0]]
            first += part_ref.shape[0]


def block_pass(
    pieces, sources, scales, scale_start, panels, part_rows, extra=(), carry=(), handed=()
):
    rows = sum(piece.shape[0] for piece in pieces)
    width, quarter = panels[0].shape

    def wide(count):
        return jax.ShapeDtypeStruct((count, 2 * quarter), jnp.bfloat16)

    hidden, own, other, *parts = pl.pallas_call(
        functools.partial(
            block_body,
            len(pieces),
            sources,
            len(extra),
            scale_start,
            column_step(width),
            len(carry),
            handed,
        ),
        out_shape=[wide(rows + len(carry) * rows), wide(rows), wide(rows)]
        + [jax.ShapeDtypeStruct((width, quarter), jnp.bfloat16)] * len(handed)
        + [jax.ShapeDtypeStruct((count, width), jnp.bfloat16) for count in part_rows],
        compiler_params=pltpu.CompilerParams(vmem_limit_bytes=LIMIT),
        cost_estimate=work(16 * rows * width * quarter, 4 * rows * width),
        name="block_pass",
    )(*pieces, *extra, scales, *panels, *carry)
    return hidden, own, other, parts


def weight_body(piece_count, grad_count, step, *refs):
    pieces, refs = refs[:piece_count], refs[piece_count:]
    grad_refs, refs = refs[:grad_count], refs[grad_count:]
    *outs, held_ref, got_held_ref, out_sems, got_sems = refs
    got_ref, outs = (None, outs) if len(outs) == 1 else (outs[0], outs[1:])
    width, columns = outs[0].shape
    chunks = width // step
    grads = joined(grad_refs, slice(None))

    def fetch(chunk):
        rows = pl.ds(chunk * step, step)
        return pltpu.make_async_copy(got_ref.at[rows, :], got_held_ref.at[rows, :], got_sems.at[chunk])

    def store(chunk):
        slot = chunk % 2
        return [
            pltpu.make_async_copy(
                held_ref.at[slot, :, pl.ds(index * columns, columns)],
                out_ref.at[pl.ds(chunk * step, step), :],
                out_sems.at[slot, index],
            )
            for index, out_ref in enumerate(outs)
        ]

    if got_ref is not None:
        for chunk in range(chunks):
            fetch(chunk).start()
    for chunk in range(chunks):
        slot = chunk % 2
        total = contract(joined(pieces, pl.ds(chunk * step, step)), grads, 0, 0)
        if got_ref is not None:
            fetch(chunk).wait()
            total = (total + f32(got_held_ref[pl.ds(chunk * step, step), :])) * (1.0 / TILE)
        if chunk >= 2:
            for copy in store(chunk - 2):
                copy.wait()
        held_ref[slot] = b16(total)
        for copy in store(chunk):
            copy.start()
    for chunk in range(max(chunks - 2, 0), chunks):
        for copy in store(chunk):
            copy.wait()


def weight_pass(width, pieces, grads, got=None):
    both = grads[0].shape[1]
    rows = sum(piece.shape[0] for piece in pieces)
    step = column_step(width)
    widths = [both] if got is None else [both // 2] * 2
    here, there = pl.BlockSpec(memory_space=pltpu.VMEM), pl.BlockSpec(memory_space=pl.ANY)
    return pl.pallas_call(
        functools.partial(weight_body, len(pieces), len(grads), step),
        in_specs=[here] * (len(pieces) + len(grads)) + ([] if got is None else [there]),
        out_specs=[there] * len(widths),
        out_shape=[jax.ShapeDtypeStruct((width, columns), jnp.bfloat16) for columns in widths],
        scratch_shapes=[
            pltpu.VMEM((2, step, both), jnp.bfloat16),
            pltpu.VMEM((step if got is None else width, both), jnp.bfloat16),
            pltpu.SemaphoreType.DMA((2, 2)),
            pltpu.SemaphoreType.DMA((width // step,)),
        ],
        compiler_params=pltpu.CompilerParams(vmem_limit_bytes=LIMIT),
        cost_estimate=work(2 * rows * width * both, 2 * width * (rows + 2 * both)),
        name="weight_pass",
    )(
        *(pltpu.with_memory_space_constraint(part, pltpu.VMEM) for part in (*pieces, *grads)),
        *([] if got is None else [got]),
    )


def join_body(home_ref, far_ref, out_ref):
    kept = out_ref.shape[0] - far_ref.shape[0]
    if kept:
        out_ref[:kept, :] = home_ref[:kept, :]
    out_ref[kept:, :] = b16(f32(home_ref[kept:, :]) + f32(far_ref[...]))


def join(home, far, cost):
    return pl.pallas_call(
        join_body,
        out_shape=jax.ShapeDtypeStruct(home.shape, home.dtype),
        compiler_params=pltpu.CompilerParams(vmem_limit_bytes=LIMIT),
        cost_estimate=cost,
        name="join",
    )(home, far)


def hidden_sum_body(near_ref, far_ref, back_ref, out_ref):
    rows, quarter = near_ref.shape[0], out_ref.shape[1]
    for block, home_ref in enumerate((near_ref, far_ref)):
        part = pl.ds(block * rows, rows)
        out_ref[part, :] = b16(f32(home_ref[:rows, quarter:]) + f32(back_ref[part, quarter:]))


def hidden_sum(near, far, back):
    rows, both = back.shape
    return pl.pallas_call(
        hidden_sum_body,
        out_shape=jax.ShapeDtypeStruct((rows, both // 2), back.dtype),
        compiler_params=pltpu.CompilerParams(vmem_limit_bytes=LIMIT),
        cost_estimate=LONG,
        name="hidden_sum",
    )(near, far, back)


def final_body(near_ref, home_ref, low_near_ref, first_ref, middle_ref, low_ref, out_ref):
    first = first_ref.shape[0]
    rest = middle_ref.shape[0]
    head = first + rest
    out_ref[:first, :] = b16(f32(near_ref[:first, :]) + f32(home_ref[...]) + f32(first_ref[...]))
    out_ref[first:head, :] = b16(
        f32(near_ref[first:head, :]) + f32(low_ref[:rest, :]) + f32(middle_ref[...])
    )
    out_ref[head:, :] = b16(
        f32(near_ref[head:, :]) + f32(low_near_ref[...]) + f32(low_ref[rest:, :])
    )


def final(near, *others):
    return pl.pallas_call(
        final_body,
        out_shape=jax.ShapeDtypeStruct(near.shape, near.dtype),
        compiler_params=pltpu.CompilerParams(vmem_limit_bytes=LIMIT),
        cost_estimate=LONG,
        name="final",
    )(near, *others)


def hidden_body(near_ref, far_ref, back_ref, got_ref, out_ref):
    rank = lax.axis_index("dp")
    _, rows, quarter = out_ref.shape
    for block, home_ref in enumerate((near_ref, far_ref)):
        part = pl.ds(block * rows, rows)
        home, back = home_ref[:rows, :quarter], back_ref[part, :quarter]
        out_ref[(2 * block) ^ rank] = b16(f32(home) + f32(back))
        out_ref[(2 * block + 1) ^ rank] = got_ref[part, :]


def hidden_pass(near, far, back, got):
    rows, both = near.shape
    return pl.pallas_call(
        hidden_body,
        out_shape=jax.ShapeDtypeStruct((4, rows, both // 2), near.dtype),
        compiler_params=pltpu.CompilerParams(vmem_limit_bytes=LIMIT),
        cost_estimate=work(0, 0),
        name="hidden_pass",
    )(near, far, back, got)


def per_device(tokens, cotangent, gate_weights, tile_expert, w_gate, w_up):
    row_count = tokens.shape[1]
    tile_count = row_count // TILE
    cycle_size = lax.axis_size("expert")
    position = lax.axis_index("expert")
    before = (position + cycle_size - 1) % cycle_size
    group_count = lax.axis_size("dp")
    rank = lax.axis_index("dp")
    quarter = w_gate.shape[2]
    out_head = OUT_SHARE * tile_count
    first, head = (share * tile_count for share in BACK_SHARE)
    tile, tile_grad = tokens[0], cotangent[0]

    def row_scale(group, place):
        owners = lax.dynamic_slice(tile_expert, (group, place * tile_count), (1, tile_count))
        weights = lax.dynamic_slice(gate_weights, (group, place * row_count), (1, row_count))
        routed = jnp.repeat(owners == position, TILE, axis=1, total_repeat_length=row_count)
        return jnp.where(routed, weights, jnp.zeros_like(weights)).reshape(row_count, 1)

    far = (rank + group_count // 2) % group_count
    scales = jnp.concatenate(
        [
            row_scale(group, place)
            for group, place in ((rank, position), (far, position), (rank, before), (far, before))
        ]
    )

    width = tile.shape[1]
    y_tile = across(tile)
    near_top, near_low, near_sent = pack(tile, tile_grad, out_head)
    x_top, x_low, y_grads = shifted(near_top, 1), shifted(near_low, 1), across(near_sent)
    panels = (w_gate[0], w_up[0], within(w_gate[0]), within(w_up[0]))
    hid_hn, own_hn, other_hn, (part_hn,) = block_pass(
        (near_top, near_low), ((0, width), (1, width)), scales, 0, panels, (row_count,)
    )
    x_top, y_grads = after((x_top, y_grads), hid_hn)
    x_sent = x_top[:, :width]
    xy_top = across(x_sent)
    y_tile = after(y_tile, x_sent)
    y_sent = y_tile[out_head:]
    xy_low = shifted(y_sent, 1)
    xy_grads = shifted(y_grads, 1)
    x_low = after(x_low, y_sent)

    lower = row_count - head
    hid_mid, own_mid, other_mid, mid_parts = block_pass(
        (y_tile, x_top, x_low),
        ((3, 0), (1, width), (2, width)),
        scales,
        row_count,
        panels,
        (first, row_count - first, first, head - first, lower),
        extra=(y_grads,),
        handed=(2, 3),
    )
    *handed, first_hf, rest_hf, first_pn, middle_pn, lower_pn = mid_parts
    first_home = across(first_hf)
    low_near = shifted(lower_pn, -1)
    xy_low, xy_top, xy_grads = after((xy_low, xy_top, xy_grads), hid_mid)
    hid_past, own_pf, other_pf, (first_pf, middle_pf, lower_pf) = block_pass(
        (xy_top, xy_low),
        ((2, 0),),
        scales,
        3 * row_count,
        (*panels[:2], *handed),
        (first, head - first, lower),
        extra=(xy_grads,),
        carry=(hid_mid,),
    )
    first_past, middle_past = across(first_pf), across(middle_pf)
    low_far = shifted(lower_pf, -1)

    pieces = (near_top, near_low, y_tile, x_top, x_low, xy_top, xy_low)
    (sent,) = weight_pass(width, pieces, after((other_hn, other_mid, other_pf), first_home, low_near))
    got = within(sent)
    hid_back = shifted(hid_past, -1)
    low_sum = join(rest_hf, after(low_far, sent), work(0, 0))
    low_home = across(low_sum)
    first_sum = join(first_pn, after(first_past, low_sum), work(0, 0))
    first_back = shifted(first_sum, -1)
    middle_sum = join(middle_pn, after(middle_past, first_sum), work(0, 0))
    middle_back = shifted(middle_sum, -1)
    hid_other = hidden_sum(hid_hn, hid_mid, after(hid_back, middle_sum))
    hid_got = within(hid_other)
    grad_gate, grad_up = weight_pass(
        width, pieces, (own_hn, own_mid, own_pf), after(got, hid_other)
    )
    hid_got = after(hid_got, grad_gate)
    hidden = hidden_pass(hid_hn, hid_mid, hid_back, hid_got)
    d_tokens = final(part_hn, first_home, low_near, after(first_back, hidden), middle_back, low_home)
    return (d_tokens[None], hidden, grad_gate[None], grad_up[None])


def solution(mesh):
    in_specs = (
        P("dp", "expert", None),
        P("dp", "expert", None),
        P(),
        P(),
        P("expert", None, "dp"),
        P("expert", None, "dp"),
    )
    out_specs = (
        P("dp", "expert", None),
        P(None, "expert", "dp"),
        P("expert", None, "dp"),
        P("expert", None, "dp"),
    )
    return jax.shard_map(
        per_device, mesh=mesh, in_specs=in_specs, out_specs=out_specs, check_vma=False
    )
```

```python
import functools

import jax
import jax.numpy as jnp
from jax import lax
from jax.experimental import pallas as pl
from jax.experimental.pallas import tpu as pltpu
from jax.sharding import PartitionSpec as P

TILE = 128
OUT_SHARE = 80
BACK_SHARE = (48, 80)
LIMIT = 20 * 2**20
LONG = pl.CostEstimate(flops=8 * 10**10, bytes_accessed=2 * 10**8, transcendentals=0)


def work(flops, moved):
    return pl.CostEstimate(flops=flops, bytes_accessed=moved, transcendentals=0)


def shifted(value, steps):
    count = lax.axis_size("expert")
    pairs = [(source, (source + steps) % count) for source in range(count)]
    return lax.ppermute(value, "expert", pairs)


def across(value):
    count = lax.axis_size("dp")
    pairs = [(source, (source + count // 2) % count) for source in range(count)]
    return lax.ppermute(value, "dp", pairs)


def within(value):
    count = lax.axis_size("dp")
    pairs = [(source, source + 1 - 2 * (source % 2)) for source in range(count)]
    return lax.ppermute(value, "dp", pairs)


def after(values, *earlier):
    return lax.optimization_barrier((values, earlier))[0]


def f32(value):
    return value.astype(jnp.float32)


def b16(value):
    return value.astype(jnp.bfloat16)


def column_step(width):
    for step in (512, 256, 128):
        if width % step == 0:
            return step
    return width


def contract(left, right, left_axis, right_axis):
    return lax.dot_general(
        left, right, (((left_axis,), (right_axis,)), ((), ())), preferred_element_type=jnp.float32
    )


def joined(refs, columns):
    return jnp.concatenate([ref[:, columns] for ref in refs], axis=0)


def pack_body(tile_ref, grads_ref, top_ref, low_ref, sent_ref):
    rank = lax.axis_index("dp")
    side, core = rank // 2, rank % 2
    width = tile_ref.shape[1]
    quarter = grads_ref.shape[1] // 4
    head = top_ref.shape[0]
    parts = [
        grads_ref[:, pl.ds(pl.multiple_of((2 * which + first) * quarter, quarter), quarter)]
        for which in (1 - side, side)
        for first in (core, 1 - core)
    ]
    sent, kept = jnp.concatenate(parts[:2], axis=1), jnp.concatenate(parts[2:], axis=1)
    sent_ref[...] = sent
    top_ref[:, :width] = tile_ref[:head, :]
    top_ref[:, width:] = kept[:head]
    low_ref[:, :width] = tile_ref[head:, :]
    low_ref[:, width:] = kept[head:]


def pack(tile, grads, head):
    rows, width = tile.shape
    whole = grads.shape[1]
    return pl.pallas_call(
        pack_body,
        out_shape=[
            jax.ShapeDtypeStruct((head, width + whole // 2), tile.dtype),
            jax.ShapeDtypeStruct((rows - head, width + whole // 2), tile.dtype),
            jax.ShapeDtypeStruct((rows, whole // 2), tile.dtype),
        ],
        compiler_params=pltpu.CompilerParams(vmem_limit_bytes=LIMIT),
        cost_estimate=work(0, 4 * rows * (width + whole)),
        name="pack",
    )(
        pltpu.with_memory_space_constraint(tile, pltpu.HBM),
        pltpu.with_memory_space_constraint(grads, pltpu.HBM),
    )


def block_body(piece_count, sources, extra, scale_start, step, carried, handed, *refs):
    held, refs = refs[: piece_count + extra], refs[piece_count + extra :]
    pieces = held[:piece_count]
    scale_ref, *panels = refs[:5]
    carry_refs, refs = refs[5 : 5 + carried], refs[5 + carried :]
    hidden_ref, own_ref, other_ref, *part_refs = refs
    for index, panel_index in enumerate(handed):
        part_refs[index][...] = panels[panel_index][...]
    part_refs = part_refs[len(handed) :]
    width, quarter = panels[0].shape
    rows = own_ref.shape[0]
    kept = hidden_ref.shape[0] - rows
    for carry_ref in carry_refs:
        hidden_ref[:kept, :] = carry_ref[pl.ds(carry_ref.shape[0] - kept, kept), :]
    values = joined(pieces, pl.ds(0, width))
    factor = scale_ref[pl.ds(scale_start, rows), :]
    grads = []
    for which, out_ref in enumerate((own_ref, other_ref)):
        gate_val = contract(values, panels[2 * which][...], 1, 0)
        up_val = contract(values, panels[2 * which + 1][...], 1, 0)
        columns = pl.ds(which * quarter, quarter)
        sigmoid_val = jax.nn.sigmoid(gate_val)
        activation = gate_val * sigmoid_val
        hidden_ref[kept:, columns] = b16(factor * activation * up_val)
        received = jnp.concatenate(
            [
                held[index][:, pl.ds(start + which * quarter, quarter)]
                for index, start in sources
            ]
        )
        act_grad = factor * f32(received)
        up_grad = b16(act_grad * activation)
        gate_grad = b16(act_grad * up_val * sigmoid_val * (1.0 + gate_val * (1.0 - sigmoid_val)))
        out_ref[:, :quarter] = gate_grad
        out_ref[:, quarter:] = up_grad
        grads += [gate_grad.T, up_grad.T]
    for start in range(0, width, step):
        columns = pl.ds(start, step)
        part = b16(
            sum(contract(panel[columns, :], grad, 1, 0) for panel, grad in zip(panels, grads))
        ).T
        first = 0
        for part_ref in part_refs:
            part_ref[:, columns] = part[first : first + part_ref.shape[0]]
            first += part_ref.shape[0]


def block_pass(
    pieces, sources, scales, scale_start, panels, part_rows, extra=(), carry=(), handed=()
):
    rows = sum(piece.shape[0] for piece in pieces)
    width, quarter = panels[0].shape

    def wide(count):
        return jax.ShapeDtypeStruct((count, 2 * quarter), jnp.bfloat16)

    hidden, own, other, *parts = pl.pallas_call(
        functools.partial(
            block_body,
            len(pieces),
            sources,
            len(extra),
            scale_start,
            column_step(width),
            len(carry),
            handed,
        ),
        out_shape=[wide(rows + len(carry) * rows), wide(rows), wide(rows)]
        + [jax.ShapeDtypeStruct((width, quarter), jnp.bfloat16)] * len(handed)
        + [jax.ShapeDtypeStruct((count, width), jnp.bfloat16) for count in part_rows],
        compiler_params=pltpu.CompilerParams(vmem_limit_bytes=LIMIT),
        cost_estimate=work(16 * rows * width * quarter, 4 * rows * width),
        name="block_pass",
    )(*pieces, *extra, scales, *panels, *carry)
    return hidden, own, other, parts


def weight_body(piece_count, grad_count, step, *refs):
    pieces, refs = refs[:piece_count], refs[piece_count:]
    grad_refs, refs = refs[:grad_count], refs[grad_count:]
    *outs, held_ref, got_held_ref, out_sems, got_sems = refs
    got_ref, outs = (None, outs) if len(outs) == 1 else (outs[0], outs[1:])
    width, columns = outs[0].shape
    chunks = width // step
    grads = joined(grad_refs, slice(None))

    def fetch(chunk):
        rows = pl.ds(chunk * step, step)
        return pltpu.make_async_copy(got_ref.at[rows, :], got_held_ref.at[rows, :], got_sems.at[chunk])

    def store(chunk):
        slot = chunk % 2
        return [
            pltpu.make_async_copy(
                held_ref.at[slot, :, pl.ds(index * columns, columns)],
                out_ref.at[pl.ds(chunk * step, step), :],
                out_sems.at[slot, index],
            )
            for index, out_ref in enumerate(outs)
        ]

    if got_ref is not None:
        for chunk in range(chunks):
            fetch(chunk).start()
    for chunk in range(chunks):
        slot = chunk % 2
        total = contract(joined(pieces, pl.ds(chunk * step, step)), grads, 0, 0)
        if got_ref is not None:
            fetch(chunk).wait()
            total = (total + f32(got_held_ref[pl.ds(chunk * step, step), :])) * (1.0 / TILE)
        if chunk >= 2:
            for copy in store(chunk - 2):
                copy.wait()
        held_ref[slot] = b16(total)
        for copy in store(chunk):
            copy.start()
    for chunk in range(max(chunks - 2, 0), chunks):
        for copy in store(chunk):
            copy.wait()


def weight_pass(width, pieces, grads, got=None):
    both = grads[0].shape[1]
    rows = sum(piece.shape[0] for piece in pieces)
    step = column_step(width)
    widths = [both] if got is None else [both // 2] * 2
    here, there = pl.BlockSpec(memory_space=pltpu.VMEM), pl.BlockSpec(memory_space=pl.ANY)
    return pl.pallas_call(
        functools.partial(weight_body, len(pieces), len(grads), step),
        in_specs=[here] * (len(pieces) + len(grads)) + ([] if got is None else [there]),
        out_specs=[there] * len(widths),
        out_shape=[jax.ShapeDtypeStruct((width, columns), jnp.bfloat16) for columns in widths],
        scratch_shapes=[
            pltpu.VMEM((2, step, both), jnp.bfloat16),
            pltpu.VMEM((step if got is None else width, both), jnp.bfloat16),
            pltpu.SemaphoreType.DMA((2, 2)),
            pltpu.SemaphoreType.DMA((width // step,)),
        ],
        compiler_params=pltpu.CompilerParams(vmem_limit_bytes=LIMIT),
        cost_estimate=work(2 * rows * width * both, 2 * width * (rows + 2 * both)),
        name="weight_pass",
    )(
        *(pltpu.with_memory_space_constraint(part, pltpu.VMEM) for part in (*pieces, *grads)),
        *([] if got is None else [got]),
    )


def join_body(home_ref, far_ref, out_ref):
    kept = out_ref.shape[0] - far_ref.shape[0]
    if kept:
        out_ref[:kept, :] = home_ref[:kept, :]
    out_ref[kept:, :] = b16(f32(home_ref[kept:, :]) + f32(far_ref[...]))


def join(home, far, cost):
    return pl.pallas_call(
        join_body,
        out_shape=jax.ShapeDtypeStruct(home.shape, home.dtype),
        compiler_params=pltpu.CompilerParams(vmem_limit_bytes=LIMIT),
        cost_estimate=cost,
        name="join",
    )(home, far)


def hidden_sum_body(near_ref, far_ref, back_ref, out_ref):
    rows, quarter = near_ref.shape[0], out_ref.shape[1]
    for block, home_ref in enumerate((near_ref, far_ref)):
        part = pl.ds(block * rows, rows)
        out_ref[part, :] = b16(f32(home_ref[:rows, quarter:]) + f32(back_ref[part, quarter:]))


def hidden_sum(near, far, back):
    rows, both = back.shape
    return pl.pallas_call(
        hidden_sum_body,
        out_shape=jax.ShapeDtypeStruct((rows, both // 2), back.dtype),
        compiler_params=pltpu.CompilerParams(vmem_limit_bytes=LIMIT),
        cost_estimate=LONG,
        name="hidden_sum",
    )(near, far, back)


def final_body(near_ref, home_ref, low_near_ref, first_ref, middle_ref, low_ref, out_ref):
    first = first_ref.shape[0]
    rest = middle_ref.shape[0]
    head = first + rest
    out_ref[:first, :] = b16(f32(near_ref[:first, :]) + f32(home_ref[...]) + f32(first_ref[...]))
    out_ref[first:head, :] = b16(
        f32(near_ref[first:head, :]) + f32(low_ref[:rest, :]) + f32(middle_ref[...])
    )
    out_ref[head:, :] = b16(
        f32(near_ref[head:, :]) + f32(low_near_ref[...]) + f32(low_ref[rest:, :])
    )


def final(near, *others):
    return pl.pallas_call(
        final_body,
        out_shape=jax.ShapeDtypeStruct(near.shape, near.dtype),
        compiler_params=pltpu.CompilerParams(vmem_limit_bytes=LIMIT),
        cost_estimate=LONG,
        name="final",
    )(near, *others)


def hidden_body(near_ref, far_ref, back_ref, got_ref, out_ref):
    rank = lax.axis_index("dp")
    _, rows, quarter = out_ref.shape
    for block, home_ref in enumerate((near_ref, far_ref)):
        part = pl.ds(block * rows, rows)
        home, back = home_ref[:rows, :quarter], back_ref[part, :quarter]
        out_ref[(2 * block) ^ rank] = b16(f32(home) + f32(back))
        out_ref[(2 * block + 1) ^ rank] = got_ref[part, :]


def hidden_pass(near, far, back, got):
    rows, both = near.shape
    return pl.pallas_call(
        hidden_body,
        out_shape=jax.ShapeDtypeStruct((4, rows, both // 2), near.dtype),
        compiler_params=pltpu.CompilerParams(vmem_limit_bytes=LIMIT),
        cost_estimate=work(0, 0),
        name="hidden_pass",
    )(near, far, back, got)


def per_device(tokens, cotangent, gate_weights, tile_expert, w_gate, w_up):
    row_count = tokens.shape[1]
    tile_count = row_count // TILE
    cycle_size = lax.axis_size("expert")
    position = lax.axis_index("expert")
    before = (position + cycle_size - 1) % cycle_size
    group_count = lax.axis_size("dp")
    rank = lax.axis_index("dp")
    quarter = w_gate.shape[2]
    out_head = OUT_SHARE * tile_count
    first, head = (share * tile_count for share in BACK_SHARE)
    tile, tile_grad = tokens[0], cotangent[0]

    def row_scale(group, place):
        owners = lax.dynamic_slice(tile_expert, (group, place * tile_count), (1, tile_count))
        weights = lax.dynamic_slice(gate_weights, (group, place * row_count), (1, row_count))
        routed = jnp.repeat(owners == position, TILE, axis=1, total_repeat_length=row_count)
        return jnp.where(routed, weights, jnp.zeros_like(weights)).reshape(row_count, 1)

    far = (rank + group_count // 2) % group_count
    scales = jnp.concatenate(
        [
            row_scale(group, place)
            for group, place in ((rank, position), (far, position), (rank, before), (far, before))
        ]
    )

    width = tile.shape[1]
    y_tile = across(tile)
    near_top, near_low, near_sent = pack(tile, tile_grad, out_head)
    x_top, x_low, y_grads = shifted(near_top, 1), shifted(near_low, 1), across(near_sent)
    panels = (w_gate[0], w_up[0], within(w_gate[0]), within(w_up[0]))
    hid_hn, own_hn, other_hn, (part_hn,) = block_pass(
        (near_top, near_low), ((0, width), (1, width)), scales, 0, panels, (row_count,)
    )
    x_top, y_grads = after((x_top, y_grads), hid_hn)
    x_sent = x_top[:, :width]
    xy_top = across(x_sent)
    y_tile = after(y_tile, x_sent)
    y_sent = y_tile[out_head:]
    xy_low = shifted(y_sent, 1)
    xy_grads = shifted(y_grads, 1)
    x_low = after(x_low, y_sent)

    lower = row_count - head
    hid_mid, own_mid, other_mid, mid_parts = block_pass(
        (y_tile, x_top, x_low),
        ((3, 0), (1, width), (2, width)),
        scales,
        row_count,
        panels,
        (first, row_count - first, first, head - first, lower),
        extra=(y_grads,),
        handed=(2, 3),
    )
    *handed, first_hf, rest_hf, first_pn, middle_pn, lower_pn = mid_parts
    first_home = across(first_hf)
    low_near = shifted(lower_pn, -1)
    xy_low, xy_top, xy_grads = after((xy_low, xy_top, xy_grads), hid_mid)
    hid_past, own_pf, other_pf, (first_pf, middle_pf, lower_pf) = block_pass(
        (xy_top, xy_low),
        ((2, 0),),
        scales,
        3 * row_count,
        (*panels[:2], *handed),
        (first, head - first, lower),
        extra=(xy_grads,),
        carry=(hid_mid,),
    )
    first_past, middle_past = across(first_pf), across(middle_pf)
    low_far = shifted(lower_pf, -1)

    pieces = (near_top, near_low, y_tile, x_top, x_low, xy_top, xy_low)
    (sent,) = weight_pass(width, pieces, after((other_hn, other_mid, other_pf), first_home))
    got = within(sent)
    hid_back = shifted(hid_past, -1)
    low_near, low_far = after((low_near, low_far), sent)
    low_sum = join(rest_hf, low_far, work(0, 0))
    low_home = across(low_sum)
    first_sum = join(first_pn, after(first_past, low_sum), work(0, 0))
    first_back = shifted(first_sum, -1)
    middle_sum = join(middle_pn, after(middle_past, first_sum), work(0, 0))
    middle_back = shifted(middle_sum, -1)
    hid_other = hidden_sum(hid_hn, hid_mid, after(hid_back, middle_sum))
    hid_got = within(hid_other)
    grad_gate, grad_up = weight_pass(
        width, pieces, (own_hn, own_mid, own_pf), after(got, hid_other)
    )
    hid_got = after(hid_got, grad_gate)
    hidden = hidden_pass(hid_hn, hid_mid, hid_back, hid_got)
    d_tokens = final(part_hn, first_home, low_near, after(first_back, hidden), middle_back, low_home)
    return (d_tokens[None], hidden, grad_gate[None], grad_up[None])


def solution(mesh):
    in_specs = (
        P("dp", "expert", None),
        P("dp", "expert", None),
        P(),
        P(),
        P("expert", None, "dp"),
        P("expert", None, "dp"),
    )
    out_specs = (
        P("dp", "expert", None),
        P(None, "expert", "dp"),
        P("expert", None, "dp"),
        P("expert", None, "dp"),
    )
    return jax.shard_map(
        per_device, mesh=mesh, in_specs=in_specs, out_specs=out_specs, check_vma=False
    )
```

```python
import functools

import jax
import jax.numpy as jnp
from jax import lax
from jax.experimental import pallas as pl
from jax.experimental.pallas import tpu as pltpu
from jax.sharding import PartitionSpec as P

TILE = 128
OUT_SHARE = 80
BACK_SHARE = (48, 80)
LIMIT = 20 * 2**20
LONG = pl.CostEstimate(flops=8 * 10**10, bytes_accessed=2 * 10**8, transcendentals=0)


def work(flops, moved):
    return pl.CostEstimate(flops=flops, bytes_accessed=moved, transcendentals=0)


def shifted(value, steps):
    count = lax.axis_size("expert")
    pairs = [(source, (source + steps) % count) for source in range(count)]
    return lax.ppermute(value, "expert", pairs)


def across(value):
    count = lax.axis_size("dp")
    pairs = [(source, (source + count // 2) % count) for source in range(count)]
    return lax.ppermute(value, "dp", pairs)


def within(value):
    count = lax.axis_size("dp")
    pairs = [(source, source + 1 - 2 * (source % 2)) for source in range(count)]
    return lax.ppermute(value, "dp", pairs)


def after(values, *earlier):
    return lax.optimization_barrier((values, earlier))[0]


def f32(value):
    return value.astype(jnp.float32)


def b16(value):
    return value.astype(jnp.bfloat16)


def column_step(width):
    for step in (512, 256, 128):
        if width % step == 0:
            return step
    return width


def contract(left, right, left_axis, right_axis):
    return lax.dot_general(
        left, right, (((left_axis,), (right_axis,)), ((), ())), preferred_element_type=jnp.float32
    )


def joined(refs, columns):
    return jnp.concatenate([ref[:, columns] for ref in refs], axis=0)


def pack_body(tile_ref, grads_ref, top_ref, low_ref, sent_ref):
    rank = lax.axis_index("dp")
    side, core = rank // 2, rank % 2
    width = tile_ref.shape[1]
    quarter = grads_ref.shape[1] // 4
    head = top_ref.shape[0]
    parts = [
        grads_ref[:, pl.ds(pl.multiple_of((2 * which + first) * quarter, quarter), quarter)]
        for which in (1 - side, side)
        for first in (core, 1 - core)
    ]
    sent, kept = jnp.concatenate(parts[:2], axis=1), jnp.concatenate(parts[2:], axis=1)
    sent_ref[...] = sent
    top_ref[:, :width] = tile_ref[:head, :]
    top_ref[:, width:] = kept[:head]
    low_ref[:, :width] = tile_ref[head:, :]
    low_ref[:, width:] = kept[head:]


def pack(tile, grads, head):
    rows, width = tile.shape
    whole = grads.shape[1]
    return pl.pallas_call(
        pack_body,
        out_shape=[
            jax.ShapeDtypeStruct((head, width + whole // 2), tile.dtype),
            jax.ShapeDtypeStruct((rows - head, width + whole // 2), tile.dtype),
            jax.ShapeDtypeStruct((rows, whole // 2), tile.dtype),
        ],
        compiler_params=pltpu.CompilerParams(vmem_limit_bytes=LIMIT),
        cost_estimate=work(0, 4 * rows * (width + whole)),
        name="pack",
    )(
        pltpu.with_memory_space_constraint(tile, pltpu.HBM),
        pltpu.with_memory_space_constraint(grads, pltpu.HBM),
    )


def block_body(piece_count, sources, extra, scale_start, step, carried, handed, *refs):
    held, refs = refs[: piece_count + extra], refs[piece_count + extra :]
    pieces = held[:piece_count]
    scale_ref, *panels = refs[:5]
    carry_refs, refs = refs[5 : 5 + carried], refs[5 + carried :]
    hidden_ref, own_ref, other_ref, *part_refs = refs
    for index, panel_index in enumerate(handed):
        part_refs[index][...] = panels[panel_index][...]
    part_refs = part_refs[len(handed) :]
    width, quarter = panels[0].shape
    rows = own_ref.shape[0]
    kept = hidden_ref.shape[0] - rows
    for carry_ref in carry_refs:
        hidden_ref[:kept, :] = carry_ref[pl.ds(carry_ref.shape[0] - kept, kept), :]
    values = joined(pieces, pl.ds(0, width))
    factor = scale_ref[pl.ds(scale_start, rows), :]
    grads = []
    for which, out_ref in enumerate((own_ref, other_ref)):
        gate_val = contract(values, panels[2 * which][...], 1, 0)
        up_val = contract(values, panels[2 * which + 1][...], 1, 0)
        columns = pl.ds(which * quarter, quarter)
        sigmoid_val = jax.nn.sigmoid(gate_val)
        activation = gate_val * sigmoid_val
        hidden_ref[kept:, columns] = b16(factor * activation * up_val)
        received = jnp.concatenate(
            [
                held[index][:, pl.ds(start + which * quarter, quarter)]
                for index, start in sources
            ]
        )
        act_grad = factor * f32(received)
        up_grad = b16(act_grad * activation)
        gate_grad = b16(act_grad * up_val * sigmoid_val * (1.0 + gate_val * (1.0 - sigmoid_val)))
        out_ref[:, :quarter] = gate_grad
        out_ref[:, quarter:] = up_grad
        grads += [gate_grad.T, up_grad.T]
    for start in range(0, width, step):
        columns = pl.ds(start, step)
        part = b16(
            sum(contract(panel[columns, :], grad, 1, 0) for panel, grad in zip(panels, grads))
        ).T
        first = 0
        for part_ref in part_refs:
            part_ref[:, columns] = part[first : first + part_ref.shape[0]]
            first += part_ref.shape[0]


def block_pass(
    pieces, sources, scales, scale_start, panels, part_rows, extra=(), carry=(), handed=()
):
    rows = sum(piece.shape[0] for piece in pieces)
    width, quarter = panels[0].shape

    def wide(count):
        return jax.ShapeDtypeStruct((count, 2 * quarter), jnp.bfloat16)

    hidden, own, other, *parts = pl.pallas_call(
        functools.partial(
            block_body,
            len(pieces),
            sources,
            len(extra),
            scale_start,
            column_step(width),
            len(carry),
            handed,
        ),
        out_shape=[wide(rows + len(carry) * rows), wide(rows), wide(rows)]
        + [jax.ShapeDtypeStruct((width, quarter), jnp.bfloat16)] * len(handed)
        + [jax.ShapeDtypeStruct((count, width), jnp.bfloat16) for count in part_rows],
        compiler_params=pltpu.CompilerParams(vmem_limit_bytes=LIMIT),
        cost_estimate=work(16 * rows * width * quarter, 4 * rows * width),
        name="block_pass",
    )(*pieces, *extra, scales, *panels, *carry)
    return hidden, own, other, parts


def weight_body(piece_count, grad_count, step, *refs):
    pieces, refs = refs[:piece_count], refs[piece_count:]
    grad_refs, refs = refs[:grad_count], refs[grad_count:]
    *outs, held_ref, got_held_ref, out_sems, got_sems = refs
    got_ref, outs = (None, outs) if len(outs) == 1 else (outs[0], outs[1:])
    width, columns = outs[0].shape
    chunks = width // step
    grads = joined(grad_refs, slice(None))

    def fetch(chunk):
        rows = pl.ds(chunk * step, step)
        return pltpu.make_async_copy(got_ref.at[rows, :], got_held_ref.at[rows, :], got_sems.at[chunk])

    def store(chunk):
        slot = chunk % 2
        return [
            pltpu.make_async_copy(
                held_ref.at[slot, :, pl.ds(index * columns, columns)],
                out_ref.at[pl.ds(chunk * step, step), :],
                out_sems.at[slot, index],
            )
            for index, out_ref in enumerate(outs)
        ]

    if got_ref is not None:
        for chunk in range(chunks):
            fetch(chunk).start()
    for chunk in range(chunks):
        slot = chunk % 2
        total = contract(joined(pieces, pl.ds(chunk * step, step)), grads, 0, 0)
        if got_ref is not None:
            fetch(chunk).wait()
            total = (total + f32(got_held_ref[pl.ds(chunk * step, step), :])) * (1.0 / TILE)
        if chunk >= 2:
            for copy in store(chunk - 2):
                copy.wait()
        held_ref[slot] = b16(total)
        for copy in store(chunk):
            copy.start()
    for chunk in range(max(chunks - 2, 0), chunks):
        for copy in store(chunk):
            copy.wait()


def weight_pass(width, pieces, grads, got=None):
    both = grads[0].shape[1]
    rows = sum(piece.shape[0] for piece in pieces)
    step = column_step(width)
    widths = [both] if got is None else [both // 2] * 2
    here, there = pl.BlockSpec(memory_space=pltpu.VMEM), pl.BlockSpec(memory_space=pl.ANY)
    return pl.pallas_call(
        functools.partial(weight_body, len(pieces), len(grads), step),
        in_specs=[here] * (len(pieces) + len(grads)) + ([] if got is None else [there]),
        out_specs=[there] * len(widths),
        out_shape=[jax.ShapeDtypeStruct((width, columns), jnp.bfloat16) for columns in widths],
        scratch_shapes=[
            pltpu.VMEM((2, step, both), jnp.bfloat16),
            pltpu.VMEM((step if got is None else width, both), jnp.bfloat16),
            pltpu.SemaphoreType.DMA((2, 2)),
            pltpu.SemaphoreType.DMA((width // step,)),
        ],
        compiler_params=pltpu.CompilerParams(vmem_limit_bytes=LIMIT),
        cost_estimate=work(2 * rows * width * both, 2 * width * (rows + 2 * both)),
        name="weight_pass",
    )(
        *(pltpu.with_memory_space_constraint(part, pltpu.VMEM) for part in (*pieces, *grads)),
        *([] if got is None else [got]),
    )


def join_body(home_ref, far_ref, out_ref):
    kept = out_ref.shape[0] - far_ref.shape[0]
    if kept:
        out_ref[:kept, :] = home_ref[:kept, :]
    out_ref[kept:, :] = b16(f32(home_ref[kept:, :]) + f32(far_ref[...]))


def join(home, far, cost):
    return pl.pallas_call(
        join_body,
        out_shape=jax.ShapeDtypeStruct(home.shape, home.dtype),
        compiler_params=pltpu.CompilerParams(vmem_limit_bytes=LIMIT),
        cost_estimate=cost,
        name="join",
    )(home, far)


def hidden_sum_body(near_ref, far_ref, back_ref, out_ref):
    rows, quarter = near_ref.shape[0], out_ref.shape[1]
    for block, home_ref in enumerate((near_ref, far_ref)):
        part = pl.ds(block * rows, rows)
        out_ref[part, :] = b16(f32(home_ref[:rows, quarter:]) + f32(back_ref[part, quarter:]))


def hidden_sum(near, far, back):
    rows, both = back.shape
    return pl.pallas_call(
        hidden_sum_body,
        out_shape=jax.ShapeDtypeStruct((rows, both // 2), back.dtype),
        compiler_params=pltpu.CompilerParams(vmem_limit_bytes=LIMIT),
        cost_estimate=LONG,
        name="hidden_sum",
    )(near, far, back)


def final_body(near_ref, home_ref, low_near_ref, first_ref, middle_ref, low_ref, out_ref):
    first = first_ref.shape[0]
    rest = middle_ref.shape[0]
    head = first + rest
    out_ref[:first, :] = b16(f32(near_ref[:first, :]) + f32(home_ref[...]) + f32(first_ref[...]))
    out_ref[first:head, :] = b16(
        f32(near_ref[first:head, :]) + f32(low_ref[:rest, :]) + f32(middle_ref[...])
    )
    out_ref[head:, :] = b16(
        f32(near_ref[head:, :]) + f32(low_near_ref[...]) + f32(low_ref[rest:, :])
    )


def final(near, *others):
    return pl.pallas_call(
        final_body,
        out_shape=jax.ShapeDtypeStruct(near.shape, near.dtype),
        compiler_params=pltpu.CompilerParams(vmem_limit_bytes=LIMIT),
        cost_estimate=LONG,
        name="final",
    )(near, *others)


def hidden_body(near_ref, far_ref, back_ref, got_ref, out_ref):
    rank = lax.axis_index("dp")
    _, rows, quarter = out_ref.shape
    for block, home_ref in enumerate((near_ref, far_ref)):
        part = pl.ds(block * rows, rows)
        home, back = home_ref[:rows, :quarter], back_ref[part, :quarter]
        out_ref[(2 * block) ^ rank] = b16(f32(home) + f32(back))
        out_ref[(2 * block + 1) ^ rank] = got_ref[part, :]


def hidden_pass(near, far, back, got):
    rows, both = near.shape
    return pl.pallas_call(
        hidden_body,
        out_shape=jax.ShapeDtypeStruct((4, rows, both // 2), near.dtype),
        compiler_params=pltpu.CompilerParams(vmem_limit_bytes=LIMIT),
        cost_estimate=work(0, 0),
        name="hidden_pass",
    )(near, far, back, got)


def per_device(tokens, cotangent, gate_weights, tile_expert, w_gate, w_up):
    row_count = tokens.shape[1]
    tile_count = row_count // TILE
    cycle_size = lax.axis_size("expert")
    position = lax.axis_index("expert")
    before = (position + cycle_size - 1) % cycle_size
    group_count = lax.axis_size("dp")
    rank = lax.axis_index("dp")
    quarter = w_gate.shape[2]
    out_head = OUT_SHARE * tile_count
    first, head = (share * tile_count for share in BACK_SHARE)
    tile, tile_grad = tokens[0], cotangent[0]

    def row_scale(group, place):
        owners = lax.dynamic_slice(tile_expert, (group, place * tile_count), (1, tile_count))
        weights = lax.dynamic_slice(gate_weights, (group, place * row_count), (1, row_count))
        routed = jnp.repeat(owners == position, TILE, axis=1, total_repeat_length=row_count)
        return jnp.where(routed, weights, jnp.zeros_like(weights)).reshape(row_count, 1)

    far = (rank + group_count // 2) % group_count
    scales = jnp.concatenate(
        [
            row_scale(group, place)
            for group, place in ((rank, position), (far, position), (rank, before), (far, before))
        ]
    )

    width = tile.shape[1]
    y_tile = across(tile)
    near_top, near_low, near_sent = pack(tile, tile_grad, out_head)
    x_top, x_low, y_grads = shifted(near_top, 1), shifted(near_low, 1), across(near_sent)
    panels = (w_gate[0], w_up[0], within(w_gate[0]), within(w_up[0]))
    hid_hn, own_hn, other_hn, (part_hn,) = block_pass(
        (near_top, near_low), ((0, width), (1, width)), scales, 0, panels, (row_count,)
    )
    x_top, y_grads = after((x_top, y_grads), hid_hn)
    x_sent = x_top[:, :width]
    xy_top = across(x_sent)
    y_tile = after(y_tile, x_sent)
    y_sent = y_tile[out_head:]
    xy_low = shifted(y_sent, 1)
    xy_grads = shifted(y_grads, 1)
    x_low = after(x_low, y_sent, y_grads)

    lower = row_count - head
    hid_mid, own_mid, other_mid, mid_parts = block_pass(
        (y_tile, x_top, x_low),
        ((3, 0), (1, width), (2, width)),
        scales,
        row_count,
        panels,
        (first, row_count - first, first, head - first, lower),
        extra=(y_grads,),
        handed=(2, 3),
    )
    *handed, first_hf, rest_hf, first_pn, middle_pn, lower_pn = mid_parts
    first_home = across(first_hf)
    low_near = shifted(lower_pn, -1)
    xy_low, xy_top, xy_grads = after((xy_low, xy_top, xy_grads), hid_mid)
    hid_past, own_pf, other_pf, (first_pf, middle_pf, lower_pf) = block_pass(
        (xy_top, xy_low),
        ((2, 0),),
        scales,
        3 * row_count,
        (*panels[:2], *handed),
        (first, head - first, lower),
        extra=(xy_grads,),
        carry=(hid_mid,),
    )
    first_past, middle_past = across(first_pf), across(middle_pf)
    low_far = shifted(lower_pf, -1)

    pieces = (near_top, near_low, y_tile, x_top, x_low, xy_top, xy_low)
    (sent,) = weight_pass(width, pieces, after((other_hn, other_mid, other_pf), first_home))
    got = within(sent)
    hid_back = shifted(hid_past, -1)
    low_near, low_far = after((low_near, low_far), sent)
    low_sum = join(rest_hf, low_far, work(0, 0))
    low_home = across(low_sum)
    first_sum = join(first_pn, after(first_past, low_sum), work(0, 0))
    first_back = shifted(first_sum, -1)
    middle_sum = join(middle_pn, after(middle_past, first_sum), work(0, 0))
    middle_back = shifted(middle_sum, -1)
    hid_other = hidden_sum(hid_hn, hid_mid, after(hid_back, middle_sum))
    hid_got = within(hid_other)
    grad_gate, grad_up = weight_pass(
        width, pieces, (own_hn, own_mid, own_pf), after(got, hid_other)
    )
    hid_got = after(hid_got, grad_gate)
    hidden = hidden_pass(hid_hn, hid_mid, hid_back, hid_got)
    d_tokens = final(part_hn, first_home, low_near, after(first_back, hidden), middle_back, low_home)
    return (d_tokens[None], hidden, grad_gate[None], grad_up[None])


def solution(mesh):
    in_specs = (
        P("dp", "expert", None),
        P("dp", "expert", None),
        P(),
        P(),
        P("expert", None, "dp"),
        P("expert", None, "dp"),
    )
    out_specs = (
        P("dp", "expert", None),
        P(None, "expert", "dp"),
        P("expert", None, "dp"),
        P("expert", None, "dp"),
    )
    return jax.shard_map(
        per_device, mesh=mesh, in_specs=in_specs, out_specs=out_specs, check_vma=False
    )
```

```python
import functools

import jax
import jax.numpy as jnp
from jax import lax
from jax.experimental import pallas as pl
from jax.experimental.pallas import tpu as pltpu
from jax.sharding import PartitionSpec as P

TILE = 128
OUT_SHARE = 80
BACK_SHARE = (48, 80)
LIMIT = 20 * 2**20
LONG = pl.CostEstimate(flops=8 * 10**10, bytes_accessed=2 * 10**8, transcendentals=0)


def work(flops, moved):
    return pl.CostEstimate(flops=flops, bytes_accessed=moved, transcendentals=0)


def shifted(value, steps):
    count = lax.axis_size("expert")
    pairs = [(source, (source + steps) % count) for source in range(count)]
    return lax.ppermute(value, "expert", pairs)


def across(value):
    count = lax.axis_size("dp")
    pairs = [(source, (source + count // 2) % count) for source in range(count)]
    return lax.ppermute(value, "dp", pairs)


def within(value):
    count = lax.axis_size("dp")
    pairs = [(source, source + 1 - 2 * (source % 2)) for source in range(count)]
    return lax.ppermute(value, "dp", pairs)


def after(values, *earlier):
    return lax.optimization_barrier((values, earlier))[0]


def f32(value):
    return value.astype(jnp.float32)


def b16(value):
    return value.astype(jnp.bfloat16)


def column_step(width):
    for step in (512, 256, 128):
        if width % step == 0:
            return step
    return width


def contract(left, right, left_axis, right_axis):
    return lax.dot_general(
        left, right, (((left_axis,), (right_axis,)), ((), ())), preferred_element_type=jnp.float32
    )


def joined(refs, columns):
    return jnp.concatenate([ref[:, columns] for ref in refs], axis=0)


def pack_body(tile_ref, grads_ref, top_ref, low_ref, sent_ref):
    rank = lax.axis_index("dp")
    side, core = rank // 2, rank % 2
    width = tile_ref.shape[1]
    quarter = grads_ref.shape[1] // 4
    head = top_ref.shape[0]
    parts = [
        grads_ref[:, pl.ds(pl.multiple_of((2 * which + first) * quarter, quarter), quarter)]
        for which in (1 - side, side)
        for first in (core, 1 - core)
    ]
    sent, kept = jnp.concatenate(parts[:2], axis=1), jnp.concatenate(parts[2:], axis=1)
    sent_ref[...] = sent
    top_ref[:, :width] = tile_ref[:head, :]
    top_ref[:, width:] = kept[:head]
    low_ref[:, :width] = tile_ref[head:, :]
    low_ref[:, width:] = kept[head:]


def pack(tile, grads, head):
    rows, width = tile.shape
    whole = grads.shape[1]
    return pl.pallas_call(
        pack_body,
        out_shape=[
            jax.ShapeDtypeStruct((head, width + whole // 2), tile.dtype),
            jax.ShapeDtypeStruct((rows - head, width + whole // 2), tile.dtype),
            jax.ShapeDtypeStruct((rows, whole // 2), tile.dtype),
        ],
        compiler_params=pltpu.CompilerParams(vmem_limit_bytes=LIMIT),
        cost_estimate=work(0, 4 * rows * (width + whole)),
        name="pack",
    )(
        pltpu.with_memory_space_constraint(tile, pltpu.HBM),
        pltpu.with_memory_space_constraint(grads, pltpu.HBM),
    )


def block_body(piece_count, sources, extra, scale_start, step, carried, handed, *refs):
    held, refs = refs[: piece_count + extra], refs[piece_count + extra :]
    pieces = held[:piece_count]
    scale_ref, *panels = refs[:5]
    carry_refs, refs = refs[5 : 5 + carried], refs[5 + carried :]
    hidden_ref, own_ref, other_ref, *part_refs = refs
    for index, panel_index in enumerate(handed):
        part_refs[index][...] = panels[panel_index][...]
    part_refs = part_refs[len(handed) :]
    width, quarter = panels[0].shape
    rows = own_ref.shape[0]
    kept = hidden_ref.shape[0] - rows
    for carry_ref in carry_refs:
        hidden_ref[:kept, :] = carry_ref[pl.ds(carry_ref.shape[0] - kept, kept), :]
    values = joined(pieces, pl.ds(0, width))
    factor = scale_ref[pl.ds(scale_start, rows), :]
    grads = []
    for which, out_ref in enumerate((own_ref, other_ref)):
        gate_val = contract(values, panels[2 * which][...], 1, 0)
        up_val = contract(values, panels[2 * which + 1][...], 1, 0)
        columns = pl.ds(which * quarter, quarter)
        sigmoid_val = jax.nn.sigmoid(gate_val)
        activation = gate_val * sigmoid_val
        hidden_ref[kept:, columns] = b16(factor * activation * up_val)
        received = jnp.concatenate(
            [
                held[index][:, pl.ds(start + which * quarter, quarter)]
                for index, start in sources
            ]
        )
        act_grad = factor * f32(received)
        up_grad = b16(act_grad * activation)
        gate_grad = b16(act_grad * up_val * sigmoid_val * (1.0 + gate_val * (1.0 - sigmoid_val)))
        out_ref[:, :quarter] = gate_grad
        out_ref[:, quarter:] = up_grad
        grads += [gate_grad.T, up_grad.T]
    for start in range(0, width, step):
        columns = pl.ds(start, step)
        part = b16(
            sum(contract(panel[columns, :], grad, 1, 0) for panel, grad in zip(panels, grads))
        ).T
        first = 0
        for part_ref in part_refs:
            part_ref[:, columns] = part[first : first + part_ref.shape[0]]
            first += part_ref.shape[0]


def block_pass(
    pieces, sources, scales, scale_start, panels, part_rows, extra=(), carry=(), handed=()
):
    rows = sum(piece.shape[0] for piece in pieces)
    width, quarter = panels[0].shape

    def wide(count):
        return jax.ShapeDtypeStruct((count, 2 * quarter), jnp.bfloat16)

    hidden, own, other, *parts = pl.pallas_call(
        functools.partial(
            block_body,
            len(pieces),
            sources,
            len(extra),
            scale_start,
            column_step(width),
            len(carry),
            handed,
        ),
        out_shape=[wide(rows + len(carry) * rows), wide(rows), wide(rows)]
        + [jax.ShapeDtypeStruct((width, quarter), jnp.bfloat16)] * len(handed)
        + [jax.ShapeDtypeStruct((count, width), jnp.bfloat16) for count in part_rows],
        compiler_params=pltpu.CompilerParams(vmem_limit_bytes=LIMIT),
        cost_estimate=work(24 * rows * width * quarter, 4 * rows * width),
        name="block_pass",
    )(*pieces, *extra, scales, *panels, *carry)
    return hidden, own, other, parts


def weight_body(piece_count, grad_count, step, *refs):
    pieces, refs = refs[:piece_count], refs[piece_count:]
    grad_refs, refs = refs[:grad_count], refs[grad_count:]
    *outs, held_ref, got_held_ref, out_sems, got_sems = refs
    got_ref, outs = (None, outs) if len(outs) == 1 else (outs[0], outs[1:])
    width, columns = outs[0].shape
    chunks = width // step
    grads = joined(grad_refs, slice(None))

    def fetch(chunk):
        rows = pl.ds(chunk * step, step)
        return pltpu.make_async_copy(got_ref.at[rows, :], got_held_ref.at[rows, :], got_sems.at[chunk])

    def store(chunk):
        slot = chunk % 2
        return [
            pltpu.make_async_copy(
                held_ref.at[slot, :, pl.ds(index * columns, columns)],
                out_ref.at[pl.ds(chunk * step, step), :],
                out_sems.at[slot, index],
            )
            for index, out_ref in enumerate(outs)
        ]

    if got_ref is not None:
        for chunk in range(chunks):
            fetch(chunk).start()
    for chunk in range(chunks):
        slot = chunk % 2
        total = contract(joined(pieces, pl.ds(chunk * step, step)), grads, 0, 0)
        if got_ref is not None:
            fetch(chunk).wait()
            total = (total + f32(got_held_ref[pl.ds(chunk * step, step), :])) * (1.0 / TILE)
        if chunk >= 2:
            for copy in store(chunk - 2):
                copy.wait()
        held_ref[slot] = b16(total)
        for copy in store(chunk):
            copy.start()
    for chunk in range(max(chunks - 2, 0), chunks):
        for copy in store(chunk):
            copy.wait()


def weight_pass(width, pieces, grads, got=None):
    both = grads[0].shape[1]
    rows = sum(piece.shape[0] for piece in pieces)
    step = column_step(width)
    widths = [both] if got is None else [both // 2] * 2
    here, there = pl.BlockSpec(memory_space=pltpu.VMEM), pl.BlockSpec(memory_space=pl.ANY)
    return pl.pallas_call(
        functools.partial(weight_body, len(pieces), len(grads), step),
        in_specs=[here] * (len(pieces) + len(grads)) + ([] if got is None else [there]),
        out_specs=[there] * len(widths),
        out_shape=[jax.ShapeDtypeStruct((width, columns), jnp.bfloat16) for columns in widths],
        scratch_shapes=[
            pltpu.VMEM((2, step, both), jnp.bfloat16),
            pltpu.VMEM((step if got is None else width, both), jnp.bfloat16),
            pltpu.SemaphoreType.DMA((2, 2)),
            pltpu.SemaphoreType.DMA((width // step,)),
        ],
        compiler_params=pltpu.CompilerParams(vmem_limit_bytes=LIMIT),
        cost_estimate=work(2 * rows * width * both, 2 * width * (rows + 2 * both)),
        name="weight_pass",
    )(
        *(pltpu.with_memory_space_constraint(part, pltpu.VMEM) for part in (*pieces, *grads)),
        *([] if got is None else [got]),
    )


def join_body(home_ref, far_ref, out_ref):
    kept = out_ref.shape[0] - far_ref.shape[0]
    if kept:
        out_ref[:kept, :] = home_ref[:kept, :]
    out_ref[kept:, :] = b16(f32(home_ref[kept:, :]) + f32(far_ref[...]))


def join(home, far, cost):
    return pl.pallas_call(
        join_body,
        out_shape=jax.ShapeDtypeStruct(home.shape, home.dtype),
        compiler_params=pltpu.CompilerParams(vmem_limit_bytes=LIMIT),
        cost_estimate=cost,
        name="join",
    )(home, far)


def hidden_sum_body(near_ref, far_ref, back_ref, out_ref):
    rows, quarter = near_ref.shape[0], out_ref.shape[1]
    for block, home_ref in enumerate((near_ref, far_ref)):
        part = pl.ds(block * rows, rows)
        out_ref[part, :] = b16(f32(home_ref[:rows, quarter:]) + f32(back_ref[part, quarter:]))


def hidden_sum(near, far, back):
    rows, both = back.shape
    return pl.pallas_call(
        hidden_sum_body,
        out_shape=jax.ShapeDtypeStruct((rows, both // 2), back.dtype),
        compiler_params=pltpu.CompilerParams(vmem_limit_bytes=LIMIT),
        cost_estimate=LONG,
        name="hidden_sum",
    )(near, far, back)


def final_body(near_ref, home_ref, low_near_ref, first_ref, middle_ref, low_ref, out_ref):
    first = first_ref.shape[0]
    rest = middle_ref.shape[0]
    head = first + rest
    out_ref[:first, :] = b16(f32(near_ref[:first, :]) + f32(home_ref[...]) + f32(first_ref[...]))
    out_ref[first:head, :] = b16(
        f32(near_ref[first:head, :]) + f32(low_ref[:rest, :]) + f32(middle_ref[...])
    )
    out_ref[head:, :] = b16(
        f32(near_ref[head:, :]) + f32(low_near_ref[...]) + f32(low_ref[rest:, :])
    )


def final(near, *others):
    return pl.pallas_call(
        final_body,
        out_shape=jax.ShapeDtypeStruct(near.shape, near.dtype),
        compiler_params=pltpu.CompilerParams(vmem_limit_bytes=LIMIT),
        cost_estimate=LONG,
        name="final",
    )(near, *others)


def hidden_body(near_ref, far_ref, back_ref, got_ref, out_ref):
    rank = lax.axis_index("dp")
    _, rows, quarter = out_ref.shape
    for block, home_ref in enumerate((near_ref, far_ref)):
        part = pl.ds(block * rows, rows)
        home, back = home_ref[:rows, :quarter], back_ref[part, :quarter]
        out_ref[(2 * block) ^ rank] = b16(f32(home) + f32(back))
        out_ref[(2 * block + 1) ^ rank] = got_ref[part, :]


def hidden_pass(near, far, back, got):
    rows, both = near.shape
    return pl.pallas_call(
        hidden_body,
        out_shape=jax.ShapeDtypeStruct((4, rows, both // 2), near.dtype),
        compiler_params=pltpu.CompilerParams(vmem_limit_bytes=LIMIT),
        cost_estimate=work(0, 0),
        name="hidden_pass",
    )(near, far, back, got)


def per_device(tokens, cotangent, gate_weights, tile_expert, w_gate, w_up):
    row_count = tokens.shape[1]
    tile_count = row_count // TILE
    cycle_size = lax.axis_size("expert")
    position = lax.axis_index("expert")
    before = (position + cycle_size - 1) % cycle_size
    group_count = lax.axis_size("dp")
    rank = lax.axis_index("dp")
    quarter = w_gate.shape[2]
    out_head = OUT_SHARE * tile_count
    first, head = (share * tile_count for share in BACK_SHARE)
    tile, tile_grad = tokens[0], cotangent[0]

    def row_scale(group, place):
        owners = lax.dynamic_slice(tile_expert, (group, place * tile_count), (1, tile_count))
        weights = lax.dynamic_slice(gate_weights, (group, place * row_count), (1, row_count))
        routed = jnp.repeat(owners == position, TILE, axis=1, total_repeat_length=row_count)
        return jnp.where(routed, weights, jnp.zeros_like(weights)).reshape(row_count, 1)

    far = (rank + group_count // 2) % group_count
    scales = jnp.concatenate(
        [
            row_scale(group, place)
            for group, place in ((rank, position), (far, position), (rank, before), (far, before))
        ]
    )

    width = tile.shape[1]
    y_tile = across(tile)
    near_top, near_low, near_sent = pack(tile, tile_grad, out_head)
    x_top, x_low, y_grads = shifted(near_top, 1), shifted(near_low, 1), across(near_sent)
    panels = (w_gate[0], w_up[0], within(w_gate[0]), within(w_up[0]))
    hid_hn, own_hn, other_hn, (part_hn,) = block_pass(
        (near_top, near_low), ((0, width), (1, width)), scales, 0, panels, (row_count,)
    )
    x_top, y_grads = after((x_top, y_grads), hid_hn)
    x_sent = x_top[:, :width]
    xy_top = across(x_sent)
    y_tile = after(y_tile, x_sent)
    y_sent = y_tile[out_head:]
    xy_low = shifted(y_sent, 1)
    xy_grads = shifted(y_grads, 1)
    x_low = after(x_low, y_sent, y_grads)

    lower = row_count - head
    hid_mid, own_mid, other_mid, mid_parts = block_pass(
        (y_tile, x_top, x_low),
        ((3, 0), (1, width), (2, width)),
        scales,
        row_count,
        panels,
        (first, row_count - first, first, head - first, lower),
        extra=(y_grads,),
        handed=(2, 3),
    )
    *handed, first_hf, rest_hf, first_pn, middle_pn, lower_pn = mid_parts
    first_home = across(first_hf)
    low_near = shifted(lower_pn, -1)
    xy_low, xy_top, xy_grads = after((xy_low, xy_top, xy_grads), hid_mid)
    hid_past, own_pf, other_pf, (first_pf, middle_pf, lower_pf) = block_pass(
        (xy_top, xy_low),
        ((2, 0),),
        scales,
        3 * row_count,
        (*panels[:2], *handed),
        (first, head - first, lower),
        extra=(xy_grads,),
        carry=(hid_mid,),
    )
    first_past, middle_past = across(first_pf), across(middle_pf)
    low_far = shifted(lower_pf, -1)

    pieces = (near_top, near_low, y_tile, x_top, x_low, xy_top, xy_low)
    (sent,) = weight_pass(width, pieces, after((other_hn, other_mid, other_pf), first_home))
    got = within(sent)
    hid_back = shifted(hid_past, -1)
    low_near, low_far = after((low_near, low_far), sent)
    low_sum = join(rest_hf, low_far, work(0, 0))
    low_home = across(low_sum)
    first_sum = join(first_pn, after(first_past, low_sum), work(0, 0))
    first_back = shifted(first_sum, -1)
    middle_sum = join(middle_pn, after(middle_past, first_sum), work(0, 0))
    middle_back = shifted(middle_sum, -1)
    hid_other = hidden_sum(hid_hn, hid_mid, after(hid_back, middle_sum))
    hid_got = within(hid_other)
    grad_gate, grad_up = weight_pass(
        width, pieces, (own_hn, own_mid, own_pf), after(got, hid_other)
    )
    hid_got = after(hid_got, grad_gate)
    hidden = hidden_pass(hid_hn, hid_mid, hid_back, hid_got)
    d_tokens = final(part_hn, first_home, low_near, after(first_back, hidden), middle_back, low_home)
    return (d_tokens[None], hidden, grad_gate[None], grad_up[None])


def solution(mesh):
    in_specs = (
        P("dp", "expert", None),
        P("dp", "expert", None),
        P(),
        P(),
        P("expert", None, "dp"),
        P("expert", None, "dp"),
    )
    out_specs = (
        P("dp", "expert", None),
        P(None, "expert", "dp"),
        P("expert", None, "dp"),
        P("expert", None, "dp"),
    )
    return jax.shard_map(
        per_device, mesh=mesh, in_specs=in_specs, out_specs=out_specs, check_vma=False
    )
```
